32 devices in a mesh: grp: 2 (over y), epoch: 4 (over x, core), asset: 4 (over z).
Axes of the slice: x: 2, y: 2, z: 4, core: 2. Of those that a mesh axis runs over, the one named last changes fastest.
Arguments:
- signals: bfloat16 [8, 1024, 256], P(('grp', 'epoch'), 'asset'), parts along dimension 0, may hold values from -6 to 6
- targets: bfloat16 [8, 1024, 256], P(('grp', 'epoch'), 'asset'), parts along dimension 0, may hold values from -6 to 6
- row_counts: int32 [8, 4], P(('grp', 'epoch'), 'asset'), parts along dimension 0, may hold values from 32 to 256, as said below
- feature_weights: bfloat16 [256, 2048], replicated, may hold values from -0.375 to 0.375
- phases: float32 [2048], replicated, may hold values from -3.140625 to 3.140625
- spread_ids: int32 [2048], replicated, may hold values from 0 to 3
Outputs:
- coefficients: float32 [8, 2048, 256], P(('grp', 'epoch'), 'asset'), parts along dimension 0
The draws below stay inside these ranges and needn't reach their ends.
There are 2 independent parts, one for each index of `grp`. The reference program is written for one: setup_inputs(seed, part) draws one part's arguments, and reference() takes and returns one part's arrays. A program takes and returns all parts, laid end to end along the dimension named above; an argument that names none is the same for every part. Nothing has to cross between parts.
Inputs may be any that keep to these rules, and one draw needn't show every extreme that they name: `row_counts`: each count is at least 32, and in every epoch some asset group has exactly 256 live rows.
All inputs are finite; a program needn't handle non-finite values.
Results may differ from the reference program's by a relative error of at most 0.0003.
Values may be sent and summed in bfloat16 or wider, within the bound.
A program may use at most 64 MiB of HBM per device.

```python
import jax
import jax.numpy as jnp
from jax import lax

F = 2048
TGT = 256
K = 256
R_DEV = 256
ITERS = 3
EPOCHS = 4
ASSETS = 4


def shared_factors(key):
    sign_key, load_key, target_key = jax.random.split(jax.random.fold_in(key, 23), 3)
    sign_bits = jax.random.randint(sign_key, (EPOCHS, ASSETS * R_DEV, 4), 0, 2)
    factor_signs = (2 * sign_bits - 1).astype(jnp.float32)
    loadings = jax.random.normal(load_key, (4, K), jnp.float32)
    target_loads = jax.random.normal(target_key, (4, TGT), jnp.float32)
    return (factor_signs, loadings, target_loads)


def draw_signals(key, part):
    factor_signs, loadings, target_loads = shared_factors(key)
    noise_key = jax.random.fold_in(key, 29)
    base_noise = jax.random.normal(noise_key, (EPOCHS, ASSETS * R_DEV, K), jnp.float32)
    strengths = (0.6, 0.8, 1.0, 1.2)
    values = base_noise
    for factor in range(4):
        values = values + strengths[factor] * factor_signs[:, :, factor:factor + 1] * loadings[factor][None, None, :]
    return jnp.clip(values, -6.0, 6.0).astype(jnp.bfloat16)


def draw_targets(key, part):
    factor_signs, loadings, target_loads = shared_factors(key)
    noise_key = jax.random.fold_in(key, 31)
    base_noise = jax.random.normal(noise_key, (EPOCHS, ASSETS * R_DEV, TGT), jnp.float32)
    strengths = (0.5, 0.6, 0.7, 0.8)
    values = base_noise
    for factor in range(4):
        values = values + strengths[factor] * factor_signs[:, :, factor:factor + 1] * target_loads[factor][None, None, :]
    return jnp.clip(values, -6.0, 6.0).astype(jnp.bfloat16)


def draw_row_counts(key, part):
    first_key, second_key = jax.random.split(jax.random.fold_in(key, 11))
    lowest = R_DEV // 8
    levels = jax.random.randint(first_key, (EPOCHS, ASSETS), 0, 1001)
    counts = lowest + (R_DEV - lowest) * (levels * levels // 1000) // 1000
    chosen = jax.random.randint(second_key, (EPOCHS, 1), 0, ASSETS)
    counts = jnp.where(jnp.arange(ASSETS)[None, :] == chosen, R_DEV, counts)
    return counts.astype(jnp.int32)


def plant(values, own_key, least, high):
    longest = values.shape.index(max(values.shape))
    spots = []
    for shift in (0, 1):
        where = [jax.random.randint(jax.random.fold_in(own_key, axis), (), 0, length) for axis, length in enumerate(values.shape)]
        where[longest] = (where[longest] + shift) % values.shape[longest]
        spots.append(tuple(where))
    return values.at[spots[0]].set(least).at[spots[1]].set(high)


def noise(own_key, dims, width, reach, held_as=jnp.bfloat16):
    result = jax.random.normal(own_key, dims, jnp.float32) * width
    return jnp.minimum(jnp.maximum(result, -reach), reach).astype(held_as)


def setup_inputs(seed: int = 0, part: int = 0) -> dict:
    key_of = jax.random.split(jax.random.key(seed), 7)
    part_splits = jax.random.split(jax.random.fold_in(key_of[6], part), 7)
    return {
        "signals": draw_signals(jax.random.fold_in(jax.random.fold_in(key_of[6], part), 71), part),
        "targets": draw_targets(jax.random.fold_in(jax.random.fold_in(key_of[6], part), 71), part),
        "row_counts": draw_row_counts(jax.random.fold_in(jax.random.fold_in(key_of[6], part), 71), part),
        "feature_weights": noise(key_of[3], (K, F), K ** -0.5, 0.375),
        "phases": jnp.clip(jax.random.uniform(key_of[4], (F,), jnp.float32, -3.140625, 3.140625), -3.140625, 3.140625),
        "spread_ids": plant(jax.random.randint(key_of[5], (F,), 0, 4), jax.random.fold_in(key_of[5], 1), 0, 3).astype(jnp.int32),
    }


ridge_penalty = 0.05
epsilon = 1e-06

def feature_scale(spread_ids):
    return (0.5 * (1.0 + jnp.where(spread_ids >= 1, 1.0, 0.0) + jnp.where(spread_ids >= 2, 2.0, 0.0) + jnp.where(spread_ids >= 3, 4.0, 0.0))).astype(jnp.float32)

def make_features(inputs, feature_weights, phases, spread_ids):
    projected = jnp.dot(inputs, feature_weights, preferred_element_type=jnp.float32)
    return jnp.sin(projected * feature_scale(spread_ids) + phases).astype(jnp.float32)

def reference(signals, targets, row_counts, feature_weights, phases, spread_ids):
    entries = F * TGT
    slot_index = jnp.arange(ASSETS * R_DEV) % R_DEV
    owner = jnp.arange(ASSETS * R_DEV) // R_DEV
    identity = jnp.eye(F, dtype=jnp.float32)

    def advance(state, inputs):
        summed, row_total = state
        rows_in, returns, counts = inputs
        features = make_features(rows_in, feature_weights, phases, spread_ids)
        live_mask = (slot_index < counts[owner])[:, None]
        features = jnp.where(live_mask, features, jnp.zeros_like(features))
        returns = jnp.where(live_mask, returns.astype(jnp.float32), jnp.zeros((), jnp.float32))
        combined = jnp.concatenate([features, returns], axis=1)
        group_features = features.reshape(ASSETS, R_DEV, F)
        group_combined = combined.reshape(ASSETS, R_DEV, F + TGT)

        def add_group(running, pieces):
            piece_features, piece_combined = pieces
            term = jnp.dot(piece_features.T, piece_combined, precision=lax.Precision.HIGHEST)
            return (running + term, None)
        epoch_terms, unused = lax.scan(add_group, jnp.zeros((F, F + TGT), jnp.float32), (group_features, group_combined))
        summed = summed + epoch_terms
        row_total = row_total + jnp.sum(counts).astype(jnp.float32)
        system = summed[:, :F] / row_total + ridge_penalty * identity
        residual = summed[:, F:] / row_total
        coef = jnp.zeros((F, TGT), jnp.float32)
        for iteration in range(ITERS):
            image = jnp.dot(system, residual, precision=lax.Precision.HIGHEST)
            res_norm = jnp.sum(residual * residual)
            res_curve = jnp.sum(residual * image)
            step_size = res_norm / entries / (res_curve / entries + epsilon)
            coef = coef + step_size * residual
            residual = residual - step_size * image
        return ((summed, row_total), jnp.sqrt(row_total) * coef)
    start_state = (jnp.zeros((F, F + TGT), jnp.float32), jnp.zeros((), jnp.float32))
    final_state, coefficients = lax.scan(advance, start_state, (signals, targets, row_counts))
    return coefficients
```

```python
import functools
import math

import jax
import jax.numpy as jnp
from jax import lax
from jax.experimental import pallas as pl
from jax.experimental.pallas import tpu as pltpu
from jax.sharding import PartitionSpec as P

ITERS = 3


ridge_penalty = 0.05
epsilon = 1e-06


def prefix(part, axis, combine, identity):
    place = lax.axis_index(axis)
    gathered = jax.tree.map(lambda a: lax.all_gather(a, axis), part)
    state = jax.tree.map(lambda a, e: jnp.zeros_like(a) + jnp.asarray(e, a.dtype), part, identity)

    def one(hop, state):
        return combine(
            state, jax.tree.map(lambda a: lax.dynamic_index_in_dim(a, hop, 0, False), gathered)
        )

    return lax.fori_loop(0, place, one, state)


def feature_scale(spread_ids):
    return (
        0.5
        * (
            1.0
            + jnp.where(spread_ids >= 1, 1.0, 0.0)
            + jnp.where(spread_ids >= 2, 2.0, 0.0)
            + jnp.where(spread_ids >= 3, 4.0, 0.0)
        )
    ).astype(jnp.float32)


def make_features(inputs, feature_weights, phases, spread_ids):
    projected = jnp.dot(inputs, feature_weights, preferred_element_type=jnp.float32)
    return jnp.sin(projected * feature_scale(spread_ids) + phases)


def add_pair(earlier, later):
    return (earlier[0] + later[0], earlier[1] + later[1])


def on_device(signals, targets, row_counts, feature_weights, phases, spread_ids):
    rows = signals.shape[1]
    width = feature_weights.shape[1]
    tgt_width = targets.shape[2]
    groups = lax.axis_size("asset")
    block_size = width // groups
    entries = width * tgt_width
    own_rows = row_counts[0, 0]
    all_counts = lax.all_gather(row_counts[0], "asset", axis=0, tiled=True)
    row_sum = jnp.sum(all_counts).astype(jnp.float32)
    inputs = signals[0]
    returns = targets[0]
    features = make_features(inputs, feature_weights, phases, spread_ids)
    live_mask = (jnp.arange(rows) < own_rows)[:, None]
    features = jnp.where(live_mask, features, jnp.zeros_like(features))
    returns = jnp.where(live_mask, returns.astype(jnp.float32), jnp.zeros((), jnp.float32))
    combined = jnp.concatenate([features, returns], axis=1)
    contract_rows = (((0,), (0,)), ((), ()))
    gram_block = lax.psum_scatter(
        lax.dot_general(features, combined, contract_rows, precision=lax.Precision.HIGHEST),
        "asset",
        scatter_dimension=0,
        tiled=True,
    )
    earlier, earlier_rows = prefix(
        (gram_block, row_sum),
        "epoch",
        add_pair,
        (jnp.zeros_like(gram_block), jnp.zeros((), jnp.float32)),
    )
    cumulative = earlier + gram_block
    row_total = earlier_rows + row_sum
    first_row = lax.axis_index("asset") * block_size
    diagonal = jnp.arange(width)[None, :] == first_row + jnp.arange(block_size)[:, None]
    system = cumulative[:, :width] / row_total + ridge_penalty * jnp.where(
        diagonal, 1.0, 0.0
    ).astype(jnp.float32)
    residual = cumulative[:, width:] / row_total
    coef = jnp.zeros((block_size, tgt_width), jnp.float32)
    for iteration in range(ITERS):
        image = jnp.zeros((block_size, tgt_width), jnp.float32) + jnp.dot(
            system,
            lax.all_gather(residual, "asset", axis=0, tiled=True),
            precision=lax.Precision.HIGHEST,
        )
        res_norm, res_curve = lax.psum(
            (jnp.sum(residual * residual), jnp.sum(residual * image)), "asset"
        )
        step_size = res_norm / entries / (res_curve / entries + epsilon)
        coef = coef + step_size * residual
        residual = residual - step_size * image
    return (jnp.sqrt(row_total) * coef)[None]


MESH = pl.DeviceIdType.MESH
MASK_ROWS = 16
COS = (
    1.0,
    -19.73920440673828,
    64.93911743164062,
    -85.45011138916016,
    60.16743087768555,
    -25.96688461303711,
    6.527706146240234,
)
NT = (((1,), (1,)), ((), ()))


def mm(a, b):
    return jnp.dot(a, b, preferred_element_type=jnp.float32)


def mm_nt(a, b):
    return lax.dot_general(a, b, NT, preferred_element_type=jnp.float32)


def split(a):
    high = a.astype(jnp.bfloat16)
    return high, (a - high.astype(jnp.float32)).astype(jnp.bfloat16)


def kernel(
    X, Z, chunk, entries,
    sig_ref, yt_ref, w_ref, sc_ref, ph_ref, out_ref,
    sig_all, yt_all, hi, lo, proj, lhs, msk, vec, coef, vs, ust, own, got, totals, got_totals,
    scal, last, outbox, landing,
    gs_send, gs_recv, gy_send, gy_recv, ex_send, ex_recv, t_send, t_recv,
    sc_send, sc_recv, la_send, la_recv, o_send, o_recv,
):
    rows, K = sig_ref.shape
    F = w_ref.shape[1]
    cols = yt_ref.shape[1] - MASK_ROWS
    C = 2 * cols
    B = X * Z
    n = B * rows
    nch = F // chunk
    f32 = jnp.float32
    epoch = lax.axis_index("epoch")
    z = lax.axis_index("asset")
    x = epoch // 2
    core = epoch % 2
    mate = 2 * x + (1 - core)

    def at(xx, cc, zz):
        return {"epoch": 2 * xx + cc, "asset": zz}

    barrier = pltpu.get_barrier_semaphore()
    peers = []
    for d in range(1, B):
        peers.append(at(lax.rem(x + d // Z, X), core, lax.rem(z + d % Z, Z)))
    for d in range(Z):
        peers.append(at(x, 1 - core, lax.rem(z + d, Z)))
    for peer in peers:
        pl.semaphore_signal(barrier, inc=1, device_id=peer, device_id_type=MESH)
    pl.semaphore_wait(barrier, len(peers))

    mine = x * Z + z

    def sig_copy(d):
        xx, zz = lax.rem(x + d // Z, X), lax.rem(z + d % Z, Z)
        return pltpu.make_async_remote_copy(
            src_ref=sig_ref, dst_ref=sig_all.at[mine],
            send_sem=gs_send.at[d], recv_sem=gs_recv.at[d],
            device_id=at(xx, core, zz), device_id_type=MESH)

    def y_copy(d):
        xx, zz = lax.rem(x + d // Z, X), lax.rem(z + d % Z, Z)
        return pltpu.make_async_remote_copy(
            src_ref=yt_ref.at[zz], dst_ref=yt_all.at[mine],
            send_sem=gy_send.at[d], recv_sem=gy_recv.at[d],
            device_id=at(xx, core, zz), device_id_type=MESH)

    for d in range(1, B):
        sig_copy(d).start()
        y_copy(d).start()
    sig_all[mine] = sig_ref[...]
    yt_all[mine] = yt_ref[z]

    def block(d, carry):
        @pl.when(d > 0)
        def _():
            sig_copy(d).wait()
            y_copy(d).wait()

        xx = lax.rem(x + X - d // Z, X)
        zz = lax.rem(z + Z - lax.rem(d, Z), Z)
        slot = xx * Z + zz
        base = pl.multiple_of(slot * rows, rows)
        live = yt_all[slot, cols:cols + MASK_ROWS, :].astype(f32)[0:1, :]
        y = yt_all[slot, 0:cols, :].astype(f32)
        for q in range(2):
            allow = jnp.where(2 * xx + core <= 2 * x + q, 1.0, 0.0).astype(f32)
            msk[q, :, pl.ds(base, rows)] = jnp.broadcast_to(live * allow, (8, rows))
            lhs[q * cols:(q + 1) * cols, pl.ds(base, rows)] = (y * allow).astype(jnp.bfloat16)
        for k in range(nch):
            part = slice(k * chunk, (k + 1) * chunk)
            proj[:, part] = mm(sig_all[slot], w_ref[:, part])
        for k in range(nch):
            part = slice(k * chunk, (k + 1) * chunk)
            scale = sc_ref[:, part]
            phase = ph_ref[:, part]

            def strip(r, carry):
                r0 = pl.multiple_of(r * 16, 16)
                t = proj[pl.ds(r0, 16), part] * scale + phase
                f = t - jnp.round(t)
                s = f * f
                acc = s * COS[-1] + COS[-2]
                for c in COS[-3::-1]:
                    acc = acc * s + c
                high, low = split(acc)
                to = pl.ds(pl.multiple_of(base + r0, 16), 16)
                hi[to, part] = high
                lo[to, part] = low
                return carry

            lax.fori_loop(0, rows // 16, strip, 0, unroll=4)
        return carry

    lax.fori_loop(0, B, block, 0)

    is_first = lax.broadcasted_iota(jnp.int32, (C, 1), 0) < cols

    def spread(a0, a1):
        return jnp.where(is_first, a0, a1)

    totals[...] = jnp.zeros_like(totals)
    for q in range(2):
        totals[q] = jnp.broadcast_to(jnp.sum(msk[q], axis=1, keepdims=True), totals.shape[1:])
    count_copy = pltpu.make_async_remote_copy(
        src_ref=totals, dst_ref=got_totals, send_sem=t_send, recv_sem=t_recv,
        device_id=at(x, 1 - core, z), device_id_type=MESH)
    count_copy.start()

    def exchange(s, k):
        return pltpu.make_async_remote_copy(
            src_ref=own.at[s, k], dst_ref=got.at[s, k],
            send_sem=ex_send.at[s, k], recv_sem=ex_recv.at[s, k],
            device_id=at(x, 1 - core, z), device_id_type=MESH)

    for k in range(nch):
        part = slice(k * chunk, (k + 1) * chunk)
        own[0, k] = mm(lhs[...], hi[:, part]) + mm(lhs[...], lo[:, part])
        exchange(0, k).start()
    count_copy.wait()
    count = [totals[q][0:1, 0:1] + got_totals[q][0:1, 0:1] for q in range(2)]
    inverse = spread(1.0 / count[0], 1.0 / count[1])

    norm = jnp.zeros((C, 1), f32)
    for k in range(nch):
        part = slice(k * chunk, (k + 1) * chunk)
        exchange(0, k).wait()
        v = (own[0, k] + got[0, k]) * inverse
        vec[:, part] = v
        high, low = split(v)
        vs[0:C, part] = high
        vs[C:2 * C, part] = low
        norm = norm + jnp.sum(v * v, axis=1, keepdims=True)

    tile_row = lax.broadcasted_iota(jnp.int32, (8, 128), 0)

    def tile(norm, curve):
        out = jnp.zeros((8, 128), f32)
        for i, a in enumerate((norm[0:cols], norm[cols:], curve[0:cols], curve[cols:])):
            out = jnp.where(tile_row == i, jnp.sum(a, axis=0, keepdims=True), out)
        return out

    def step_of(a):
        res_norm = spread(a[0:1, 0:1], a[1:2, 0:1])
        res_curve = spread(a[2:3, 0:1], a[3:4, 0:1])
        return res_norm / entries / (res_curve / entries + epsilon)

    for it in range(ITERS):
        final = it == ITERS - 1

        def forward(j, total):
            base = pl.multiple_of(j * rows, rows)
            here = pl.ds(base, rows)
            u = mm_nt(vs[...], hi[here, :])
            u = u[0:C] + u[C:] + mm_nt(vs[0:C, :], lo[here, :])
            u = jnp.concatenate(
                [u[0:cols] * msk[0, 0:1, here], u[cols:] * msk[1, 0:1, here]], axis=0)
            if final:
                return total + jnp.sum(u * u, axis=1, keepdims=True)
            high, low = split(u)
            ust[0:C, here] = high
            ust[C:2 * C, here] = low
            return total

        square = lax.fori_loop(0, B, forward, jnp.zeros((C, 1), f32))
        if final:
            last[core * Z + z] = tile(norm, square)
            copies = []
            for d in range(1, 2 * Z):
                cc, zz = lax.rem(core + d // Z, 2), lax.rem(z + d % Z, Z)
                copies.append(pltpu.make_async_remote_copy(
                    src_ref=last.at[core * Z + z], dst_ref=last.at[core * Z + z],
                    send_sem=la_send.at[d], recv_sem=la_recv.at[d],
                    device_id=at(x, cc, zz), device_id_type=MESH))
            for copy in copies:
                copy.start()
            for copy in copies:
                copy.wait()
            a = last[0]
            for i in range(1, 2 * Z):
                a = a + last[i]
            norms = spread(a[0:1, 0:1], a[1:2, 0:1]) * 0.5
            curve = spread(a[2:3, 0:1] / count[0], a[3:4, 0:1] / count[1]) + ridge_penalty * norms
            step = norms / entries / (curve / entries + epsilon)
            root = spread(jnp.sqrt(count[0]), jnp.sqrt(count[1]))
            for k in range(nch):
                part = slice(k * chunk, (k + 1) * chunk)
                coef[:, part] = (coef[:, part] + step * vec[:, part]) * root
        else:
            s = it + 1
            for k in range(nch):
                part = slice(k * chunk, (k + 1) * chunk)
                image = mm(ust[...], hi[:, part])
                own[s, k] = image[0:C] + image[C:] + mm(ust[0:C, :], lo[:, part])
                exchange(s, k).start()
            curve = jnp.zeros((C, 1), f32)
            for k in range(nch):
                part = slice(k * chunk, (k + 1) * chunk)
                exchange(s, k).wait()
                v = vec[:, part]
                image = (own[s, k] + got[s, k]) * inverse + ridge_penalty * v
                proj[0:C, part] = image
                curve = curve + jnp.sum(v * image, axis=1, keepdims=True)
            scal[it, z] = tile(norm, curve)
            copies = []
            for d in range(1, Z):
                copies.append(pltpu.make_async_remote_copy(
                    src_ref=scal.at[it, z], dst_ref=scal.at[it, z],
                    send_sem=sc_send.at[it, d], recv_sem=sc_recv.at[it, d],
                    device_id=at(x, core, lax.rem(z + d, Z)), device_id_type=MESH))
            for copy in copies:
                copy.start()
            for copy in copies:
                copy.wait()
            a = scal[it, 0]
            for i in range(1, Z):
                a = a + scal[it, i]
            step = step_of(a)
            norm = jnp.zeros((C, 1), f32)
            for k in range(nch):
                part = slice(k * chunk, (k + 1) * chunk)
                v = vec[:, part]
                coef[:, part] = step * v if it == 0 else coef[:, part] + step * v
                v = v - step * proj[0:C, part]
                vec[:, part] = v
                high, low = split(v)
                vs[0:C, part] = high
                vs[C:2 * C, part] = low
                norm = norm + jnp.sum(v * v, axis=1, keepdims=True)

    width = F // Z
    first = pl.multiple_of(core * cols, cols)
    for b in range(Z):
        outbox[b] = coef[pl.ds(first, cols), b * width:(b + 1) * width]
    copies = []
    for d in range(1, Z):
        zz = lax.rem(z + d, Z)
        copies.append(pltpu.make_async_remote_copy(
            src_ref=outbox.at[zz], dst_ref=landing.at[z],
            send_sem=o_send.at[d], recv_sem=o_recv.at[d],
            device_id=at(x, core, zz), device_id_type=MESH))
    for copy in copies:
        copy.start()
    landing[z] = outbox[z]
    for copy in copies:
        copy.wait()
    out_ref[...] = landing[...].reshape(Z * cols, width)


def scratch_of(X, Z, rows, K, F, cols, chunk):
    B = X * Z
    n = B * rows
    C = 2 * cols
    nch = F // chunk
    f32, bf16 = jnp.float32, jnp.bfloat16
    buffers = [
        ((B, rows, K), bf16), ((B, cols + MASK_ROWS, rows), bf16),
        ((n, F), bf16), ((n, F), bf16), ((max(rows, C), F), f32), ((C, n), bf16),
        ((2, 8, n), f32), ((C, F), f32), ((C, F), f32), ((2 * C, F), bf16), ((2 * C, n), bf16),
        ((ITERS, nch, C, chunk), f32), ((ITERS, nch, C, chunk), f32),
        ((2, 8, 128), f32), ((2, 8, 128), f32),
        ((ITERS, Z, 8, 128), f32), ((2 * Z, 8, 128), f32),
        ((Z, cols, F // Z), f32), ((Z, cols, F // Z), f32),
    ]
    held = sum(math.prod(shape) * jnp.dtype(dtype).itemsize for shape, dtype in buffers)
    sems = [(B,)] * 4 + [(ITERS, nch)] * 2 + [()] * 2 + [(ITERS, Z)] * 2 + [(2 * Z,)] * 2 + [(Z,)] * 2
    return buffers, sems, held


VMEM_BUDGET = 44 * 2**20


def plan(E, Z, rows, K, F, T):
    if E % 2 or T % Z or F % Z:
        return None
    cols, chunk = T // Z, 512
    if cols % 16 or rows % 128 or F % chunk or (F // Z) % 128 or K % 128:
        return None
    buffers, sems, held = scratch_of(E // 2, Z, rows, K, F, cols, chunk)
    if held > VMEM_BUDGET:
        return None
    return cols, chunk, buffers, sems


def fused(signals, targets, row_counts, feature_weights, phases, spread_ids):
    E, Z = lax.axis_size("epoch"), lax.axis_size("asset")
    rows, K = signals.shape[1:]
    F = feature_weights.shape[1]
    T = targets.shape[2]
    cols, chunk, buffers, sems = plan(E, Z, rows, K, F, T)
    live = jnp.arange(rows) < row_counts[0, 0]
    returns = jnp.where(live[:, None], targets[0], jnp.zeros((), targets.dtype)).T
    returns = returns.reshape(Z, cols, rows)
    mask = jnp.broadcast_to(live.astype(targets.dtype), (Z, MASK_ROWS, rows))
    returns = jnp.concatenate([returns, mask], axis=1)
    turn = 1.0 / (2.0 * math.pi)
    scale = (feature_scale(spread_ids) * turn)[None, :]
    phase = (phases * turn - 0.25)[None, :]
    vmem = pl.BlockSpec(memory_space=pltpu.VMEM)
    out = pl.pallas_call(
        functools.partial(kernel, E // 2, Z, chunk, float(F * T)),
        out_shape=jax.ShapeDtypeStruct((T, F // Z), jnp.float32),
        in_specs=[vmem] * 5,
        out_specs=vmem,
        scratch_shapes=[pltpu.VMEM(s, d) for s, d in buffers]
        + [pltpu.SemaphoreType.DMA(s) if s else pltpu.SemaphoreType.DMA for s in sems],
        compiler_params=pltpu.CompilerParams(
            collective_id=0, has_side_effects=True, vmem_limit_bytes=56 * 2**20),
    )(signals[0], returns, feature_weights, scale, phase)
    return out.T[None]


def solution(mesh):
    def run(signals, targets, row_counts, feature_weights, phases, spread_ids):
        fits = plan(
            mesh.shape["epoch"], mesh.shape["asset"], signals.shape[1],
            signals.shape[2], feature_weights.shape[1], targets.shape[2])
        body = fused if fits else on_device
        return body(signals, targets, row_counts, feature_weights, phases, spread_ids)

    placed = (
        P(("grp", "epoch"), "asset", None),
        P(("grp", "epoch"), "asset", None),
        P(("grp", "epoch"), "asset"),
        P(),
        P(),
        P(),
    )
    return jax.shard_map(
        run,
        mesh=mesh,
        in_specs=placed,
        out_specs=P(("grp", "epoch"), "asset", None),
        check_vma=False,
    )
```

```python
import functools
import math

import jax
import jax.numpy as jnp
from jax import lax
from jax.experimental import pallas as pl
from jax.experimental.pallas import tpu as pltpu
from jax.sharding import PartitionSpec as P

ITERS = 3


ridge_penalty = 0.05
epsilon = 1e-06


def prefix(part, axis, combine, identity):
    place = lax.axis_index(axis)
    gathered = jax.tree.map(lambda a: lax.all_gather(a, axis), part)
    state = jax.tree.map(lambda a, e: jnp.zeros_like(a) + jnp.asarray(e, a.dtype), part, identity)

    def one(hop, state):
        return combine(
            state, jax.tree.map(lambda a: lax.dynamic_index_in_dim(a, hop, 0, False), gathered)
        )

    return lax.fori_loop(0, place, one, state)


def feature_scale(spread_ids):
    return (
        0.5
        * (
            1.0
            + jnp.where(spread_ids >= 1, 1.0, 0.0)
            + jnp.where(spread_ids >= 2, 2.0, 0.0)
            + jnp.where(spread_ids >= 3, 4.0, 0.0)
        )
    ).astype(jnp.float32)


def make_features(inputs, feature_weights, phases, spread_ids):
    projected = jnp.dot(inputs, feature_weights, preferred_element_type=jnp.float32)
    return jnp.sin(projected * feature_scale(spread_ids) + phases)


def add_pair(earlier, later):
    return (earlier[0] + later[0], earlier[1] + later[1])


def on_device(signals, targets, row_counts, feature_weights, phases, spread_ids):
    rows = signals.shape[1]
    width = feature_weights.shape[1]
    tgt_width = targets.shape[2]
    groups = lax.axis_size("asset")
    block_size = width // groups
    entries = width * tgt_width
    own_rows = row_counts[0, 0]
    all_counts = lax.all_gather(row_counts[0], "asset", axis=0, tiled=True)
    row_sum = jnp.sum(all_counts).astype(jnp.float32)
    inputs = signals[0]
    returns = targets[0]
    features = make_features(inputs, feature_weights, phases, spread_ids)
    live_mask = (jnp.arange(rows) < own_rows)[:, None]
    features = jnp.where(live_mask, features, jnp.zeros_like(features))
    returns = jnp.where(live_mask, returns.astype(jnp.float32), jnp.zeros((), jnp.float32))
    combined = jnp.concatenate([features, returns], axis=1)
    contract_rows = (((0,), (0,)), ((), ()))
    gram_block = lax.psum_scatter(
        lax.dot_general(features, combined, contract_rows, precision=lax.Precision.HIGHEST),
        "asset",
        scatter_dimension=0,
        tiled=True,
    )
    earlier, earlier_rows = prefix(
        (gram_block, row_sum),
        "epoch",
        add_pair,
        (jnp.zeros_like(gram_block), jnp.zeros((), jnp.float32)),
    )
    cumulative = earlier + gram_block
    row_total = earlier_rows + row_sum
    first_row = lax.axis_index("asset") * block_size
    diagonal = jnp.arange(width)[None, :] == first_row + jnp.arange(block_size)[:, None]
    system = cumulative[:, :width] / row_total + ridge_penalty * jnp.where(
        diagonal, 1.0, 0.0
    ).astype(jnp.float32)
    residual = cumulative[:, width:] / row_total
    coef = jnp.zeros((block_size, tgt_width), jnp.float32)
    for iteration in range(ITERS):
        image = jnp.zeros((block_size, tgt_width), jnp.float32) + jnp.dot(
            system,
            lax.all_gather(residual, "asset", axis=0, tiled=True),
            precision=lax.Precision.HIGHEST,
        )
        res_norm, res_curve = lax.psum(
            (jnp.sum(residual * residual), jnp.sum(residual * image)), "asset"
        )
        step_size = res_norm / entries / (res_curve / entries + epsilon)
        coef = coef + step_size * residual
        residual = residual - step_size * image
    return (jnp.sqrt(row_total) * coef)[None]


MESH = pl.DeviceIdType.MESH
MASK_ROWS = 16
COS = (
    0.9999992251396179,
    -19.738977432250977,
    64.9285888671875,
    -85.27084350585938,
    58.78694152832031,
    -21.0654296875,
)
ROUNDER = 1.5 * 2.0**23
NT = (((1,), (1,)), ((), ()))


def mm(a, b):
    return jnp.dot(a, b, preferred_element_type=jnp.float32)


def mm_nt(a, b):
    return lax.dot_general(a, b, NT, preferred_element_type=jnp.float32)


def split(a):
    high = a.astype(jnp.bfloat16)
    return high, (a - high.astype(jnp.float32)).astype(jnp.bfloat16)


def kernel(
    X, Z, chunk, entries,
    counts_ref, sig_ref, y_ref, w_ref, ids_ref, phases_ref, out_ref,
    yt_own, sc_ref, ph_ref,
    sig_all, yt_all, hi, lo, proj, lhs, msk, vec, coef, vs, ust, own, got, totals, got_totals,
    scal, last, outbox, landing,
    gs_send, gs_recv, gy_send, gy_recv, fs_send, fs_recv, fy_send, fy_recv,
    ex_send, ex_recv, t_send, t_recv,
    sc_send, sc_recv, la_send, la_recv, o_send, o_recv,
):
    rows, K = sig_ref.shape
    F = w_ref.shape[1]
    cols = y_ref.shape[1] // Z
    C = 2 * cols
    B = X * Z
    n = B * rows
    nch = F // chunk
    f32 = jnp.float32
    epoch = lax.axis_index("epoch")
    z = lax.axis_index("asset")
    x = epoch // 2
    core = epoch % 2

    def at(xx, cc, zz):
        return {"epoch": 2 * xx + cc, "asset": zz}

    def signal(peer):
        pl.semaphore_signal(barrier, inc=1, device_id=peer, device_id_type=MESH)

    barrier = pltpu.get_barrier_semaphore()
    for d in range(1, Z):
        signal(at(x, core, lax.rem(z + d, Z)))
    for d in range(Z):
        signal(at(x, 1 - core, lax.rem(z + d, Z)))

    beside = sorted({1 % X, X - 1} - {0})
    for d in beside:
        signal(at(lax.rem(x + d, X), core, z))

    count_here = counts_ref[0, 0]
    alive = lax.broadcasted_iota(jnp.int32, (rows, 1), 0) < count_here
    y = jnp.where(alive, y_ref[...].astype(f32), 0.0).T
    alive = lax.broadcasted_iota(jnp.int32, (MASK_ROWS, rows), 1) < count_here
    mask = jnp.where(alive, 1.0, 0.0).astype(jnp.bfloat16)
    for b in range(Z):
        yt_own[b, 0:cols, :] = y[b * cols:(b + 1) * cols].astype(jnp.bfloat16)
        yt_own[b, cols:cols + MASK_ROWS, :] = mask
    turn = 1.0 / (2.0 * math.pi)
    sc_ref[...] = feature_scale(ids_ref[...]) * turn
    ph_ref[...] = phases_ref[...] * turn - 0.25

    pl.semaphore_wait(barrier, 2 * Z - 1 + len(beside))

    mine = x * Z + z

    def along(d):
        zz = lax.rem(z + d, Z)
        return (
            pltpu.make_async_remote_copy(
                src_ref=sig_ref, dst_ref=sig_all.at[mine],
                send_sem=gs_send.at[d], recv_sem=gs_recv.at[d],
                device_id=at(x, core, zz), device_id_type=MESH),
            pltpu.make_async_remote_copy(
                src_ref=yt_own.at[zz], dst_ref=yt_all.at[mine],
                send_sem=gy_send.at[d], recv_sem=gy_recv.at[d],
                device_id=at(x, core, zz), device_id_type=MESH),
        )

    def upward(slot):
        return (
            pltpu.make_async_remote_copy(
                src_ref=sig_all.at[slot], dst_ref=sig_all.at[slot],
                send_sem=fs_send.at[slot], recv_sem=fs_recv.at[slot],
                device_id=at(x + 1, core, z), device_id_type=MESH),
            pltpu.make_async_remote_copy(
                src_ref=yt_all.at[slot], dst_ref=yt_all.at[slot],
                send_sem=fy_send.at[slot], recv_sem=fy_recv.at[slot],
                device_id=at(x + 1, core, z), device_id_type=MESH),
        )

    for d in range(1, Z):
        for copy in along(d):
            copy.start()
    sig_all[mine] = sig_ref[...]
    yt_all[mine] = yt_own[z]

    def block(dz, dx):
        xx = x - dx
        zz = lax.rem(z + Z - dz, Z)
        slot = xx * Z + zz

        @pl.when((dx == 0) & (dz > 0))
        def _():
            for copy in along(dz):
                copy.wait()

        @pl.when(dx > 0)
        def _():
            for copy in upward(slot):
                copy.wait_recv()

        @pl.when(x < X - 1)
        def _():
            for copy in upward(slot):
                copy.start()

        base = pl.multiple_of(slot * rows, rows)
        live = yt_all[slot, cols:cols + MASK_ROWS, :].astype(f32)[0:1, :]
        y = yt_all[slot, 0:cols, :].astype(f32)
        for q in range(2):
            allow = jnp.where(2 * xx + core <= 2 * x + q, 1.0, 0.0).astype(f32)
            msk[q, :, pl.ds(base, rows)] = jnp.broadcast_to(live * allow, (8, rows))
            lhs[q * cols:(q + 1) * cols, pl.ds(base, rows)] = (y * allow).astype(jnp.bfloat16)
        for k in range(nch):
            part = slice(k * chunk, (k + 1) * chunk)
            proj[:, part] = mm(sig_all[slot], w_ref[:, part])
        for k in range(nch):
            part = slice(k * chunk, (k + 1) * chunk)
            scale = sc_ref[:, part]
            phase = ph_ref[:, part]

            def strip(r, carry):
                r0 = pl.multiple_of(r * 16, 16)
                t = proj[pl.ds(r0, 16), part] * scale + phase
                f = t - ((t + ROUNDER) - ROUNDER)
                s = f * f
                acc = s * COS[-1] + COS[-2]
                for c in COS[-3::-1]:
                    acc = acc * s + c
                high, low = split(acc)
                to = pl.ds(pl.multiple_of(base + r0, 16), 16)
                hi[to, part] = high
                lo[to, part] = low
                return carry

            lax.fori_loop(0, rows // 16, strip, 0, unroll=4)

    def column(dz, carry):
        def one(dx, carry):
            block(dz, dx)
            return carry

        return lax.fori_loop(0, x + 1, one, carry)

    lax.fori_loop(0, Z, column, 0)

    def absent(slot, carry):
        here = pl.ds(pl.multiple_of(slot * rows, rows), rows)
        hi[here, :] = jnp.zeros((rows, F), jnp.bfloat16)
        lo[here, :] = jnp.zeros((rows, F), jnp.bfloat16)
        msk[:, :, here] = jnp.zeros((2, 8, rows), f32)
        lhs[:, here] = jnp.zeros((C, rows), jnp.bfloat16)
        return carry

    lax.fori_loop((x + 1) * Z, B, absent, 0)

    @pl.when(x < X - 1)
    def _():
        def sent(slot, carry):
            for copy in upward(slot):
                copy.wait_send()
            return carry

        lax.fori_loop(0, (x + 1) * Z, sent, 0)

    is_first = lax.broadcasted_iota(jnp.int32, (C, 1), 0) < cols

    def spread(a0, a1):
        return jnp.where(is_first, a0, a1)

    totals[...] = jnp.zeros_like(totals)
    for q in range(2):
        totals[q] = jnp.broadcast_to(jnp.sum(msk[q], axis=1, keepdims=True), totals.shape[1:])
    count_copy = pltpu.make_async_remote_copy(
        src_ref=totals, dst_ref=got_totals, send_sem=t_send, recv_sem=t_recv,
        device_id=at(x, 1 - core, z), device_id_type=MESH)
    count_copy.start()

    def exchange(s, k):
        return pltpu.make_async_remote_copy(
            src_ref=own.at[s, k], dst_ref=got.at[s, k],
            send_sem=ex_send.at[s, k], recv_sem=ex_recv.at[s, k],
            device_id=at(x, 1 - core, z), device_id_type=MESH)

    for k in range(nch):
        part = slice(k * chunk, (k + 1) * chunk)
        own[0, k] = mm(lhs[...], hi[:, part]) + mm(lhs[...], lo[:, part])
        exchange(0, k).start()
    count_copy.wait()
    count = [totals[q][0:1, 0:1] + got_totals[q][0:1, 0:1] for q in range(2)]
    inverse = spread(1.0 / count[0], 1.0 / count[1])

    norm = jnp.zeros((C, 1), f32)
    for k in range(nch):
        part = slice(k * chunk, (k + 1) * chunk)
        exchange(0, k).wait()
        v = (own[0, k] + got[0, k]) * inverse
        vec[:, part] = v
        high, low = split(v)
        vs[0:C, part] = high
        vs[C:2 * C, part] = low
        norm = norm + jnp.sum(v * v, axis=1, keepdims=True)

    tile_row = lax.broadcasted_iota(jnp.int32, (8, 128), 0)

    def tile(norm, curve):
        out = jnp.zeros((8, 128), f32)
        for i, a in enumerate((norm[0:cols], norm[cols:], curve[0:cols], curve[cols:])):
            out = jnp.where(tile_row == i, jnp.sum(a, axis=0, keepdims=True), out)
        return out

    def step_of(a):
        res_norm = spread(a[0:1, 0:1], a[1:2, 0:1])
        res_curve = spread(a[2:3, 0:1], a[3:4, 0:1])
        return res_norm / entries / (res_curve / entries + epsilon)

    for it in range(ITERS):
        final = it == ITERS - 1

        def forward(j, total):
            base = pl.multiple_of(j * rows, rows)
            here = pl.ds(base, rows)
            if final:
                u = mm_nt(vs[0:C, :], hi[here, :])
            else:
                u = mm_nt(vs[...], hi[here, :])
                u = u[0:C] + u[C:]
            u = jnp.concatenate(
                [u[0:cols] * msk[0, 0:1, here], u[cols:] * msk[1, 0:1, here]], axis=0)
            if final:
                return total + jnp.sum(u * u, axis=1, keepdims=True)
            high, low = split(u)
            ust[0:C, here] = high
            ust[C:2 * C, here] = low
            return total

        square = lax.fori_loop(0, B, forward, jnp.zeros((C, 1), f32))
        if final:
            last[core * Z + z] = tile(norm, square)
            copies = []
            for d in range(1, 2 * Z):
                cc, zz = lax.rem(core + d // Z, 2), lax.rem(z + d % Z, Z)
                copies.append(pltpu.make_async_remote_copy(
                    src_ref=last.at[core * Z + z], dst_ref=last.at[core * Z + z],
                    send_sem=la_send.at[d], recv_sem=la_recv.at[d],
                    device_id=at(x, cc, zz), device_id_type=MESH))
            for copy in copies:
                copy.start()
            for copy in copies:
                copy.wait()
            a = last[0]
            for i in range(1, 2 * Z):
                a = a + last[i]
            norms = spread(a[0:1, 0:1], a[1:2, 0:1]) * 0.5
            curve = spread(a[2:3, 0:1] / count[0], a[3:4, 0:1] / count[1]) + ridge_penalty * norms
            step = norms / entries / (curve / entries + epsilon)
            root = spread(jnp.sqrt(count[0]), jnp.sqrt(count[1]))
            for k in range(nch):
                part = slice(k * chunk, (k + 1) * chunk)
                coef[:, part] = (coef[:, part] + step * vec[:, part]) * root
        else:
            s = it + 1
            for k in range(nch):
                part = slice(k * chunk, (k + 1) * chunk)
                image = mm(ust[...], hi[:, part])
                own[s, k] = image[0:C] + image[C:] + mm(ust[0:C, :], lo[:, part])
                exchange(s, k).start()
            curve = jnp.zeros((C, 1), f32)
            for k in range(nch):
                part = slice(k * chunk, (k + 1) * chunk)
                exchange(s, k).wait()
                v = vec[:, part]
                image = (own[s, k] + got[s, k]) * inverse + ridge_penalty * v
                proj[0:C, part] = image
                curve = curve + jnp.sum(v * image, axis=1, keepdims=True)
            scal[it, z] = tile(norm, curve)
            copies = []
            for d in range(1, Z):
                copies.append(pltpu.make_async_remote_copy(
                    src_ref=scal.at[it, z], dst_ref=scal.at[it, z],
                    send_sem=sc_send.at[it, d], recv_sem=sc_recv.at[it, d],
                    device_id=at(x, core, lax.rem(z + d, Z)), device_id_type=MESH))
            for copy in copies:
                copy.start()
            for copy in copies:
                copy.wait()
            a = scal[it, 0]
            for i in range(1, Z):
                a = a + scal[it, i]
            step = step_of(a)
            norm = jnp.zeros((C, 1), f32)
            for k in range(nch):
                part = slice(k * chunk, (k + 1) * chunk)
                v = vec[:, part]
                coef[:, part] = step * v if it == 0 else coef[:, part] + step * v
                v = v - step * proj[0:C, part]
                vec[:, part] = v
                high, low = split(v)
                vs[0:C, part] = high
                vs[C:2 * C, part] = low
                norm = norm + jnp.sum(v * v, axis=1, keepdims=True)

    width = F // Z
    first = pl.multiple_of(core * cols, cols)
    for b in range(Z):
        outbox[b] = coef[pl.ds(first, cols), b * width:(b + 1) * width]
    copies = []
    for d in range(1, Z):
        zz = lax.rem(z + d, Z)
        copies.append(pltpu.make_async_remote_copy(
            src_ref=outbox.at[zz], dst_ref=landing.at[z],
            send_sem=o_send.at[d], recv_sem=o_recv.at[d],
            device_id=at(x, core, zz), device_id_type=MESH))
    for copy in copies:
        copy.start()
    landing[z] = outbox[z]
    for copy in copies:
        copy.wait()
    out_ref[...] = landing[...].reshape(Z * cols, width).T


def scratch_of(X, Z, rows, K, F, cols, chunk):
    B = X * Z
    n = B * rows
    C = 2 * cols
    nch = F // chunk
    f32, bf16 = jnp.float32, jnp.bfloat16
    buffers = [
        ((Z, cols + MASK_ROWS, rows), bf16), ((1, F), f32), ((1, F), f32),
        ((B, rows, K), bf16), ((B, cols + MASK_ROWS, rows), bf16),
        ((n, F), bf16), ((n, F), bf16), ((max(rows, C), F), f32), ((C, n), bf16),
        ((2, 8, n), f32), ((C, F), f32), ((C, F), f32), ((2 * C, F), bf16), ((2 * C, n), bf16),
        ((ITERS, nch, C, chunk), f32), ((ITERS, nch, C, chunk), f32),
        ((2, 8, 128), f32), ((2, 8, 128), f32),
        ((ITERS, Z, 8, 128), f32), ((2 * Z, 8, 128), f32),
        ((Z, cols, F // Z), f32), ((Z, cols, F // Z), f32),
    ]
    held = sum(math.prod(shape) * jnp.dtype(dtype).itemsize for shape, dtype in buffers)
    sems = [(Z,)] * 4 + [(B,)] * 4 + [(ITERS, nch)] * 2 + [()] * 2 + [(ITERS, Z)] * 2 + [(2 * Z,)] * 2 + [(Z,)] * 2
    return buffers, sems, held


VMEM_BUDGET = 44 * 2**20


def plan(E, Z, rows, K, F, T):
    if E % 2 or T % Z or F % Z:
        return None
    cols, chunk = T // Z, 512
    if cols % 16 or rows % 128 or F % chunk or (F // Z) % 128 or K % 128:
        return None
    buffers, sems, held = scratch_of(E // 2, Z, rows, K, F, cols, chunk)
    if held > VMEM_BUDGET:
        return None
    return cols, chunk, buffers, sems


def fused(signals, targets, row_counts, feature_weights, phases, spread_ids):
    E, Z = lax.axis_size("epoch"), lax.axis_size("asset")
    rows, K = signals.shape[1:]
    F = feature_weights.shape[1]
    T = targets.shape[2]
    cols, chunk, buffers, sems = plan(E, Z, rows, K, F, T)
    vmem = pl.BlockSpec(memory_space=pltpu.VMEM)
    out = pl.pallas_call(
        functools.partial(kernel, E // 2, Z, chunk, float(F * T)),
        out_shape=jax.ShapeDtypeStruct((F // Z, T), jnp.float32),
        in_specs=[pl.BlockSpec(memory_space=pltpu.SMEM)] + [vmem] * 5,
        out_specs=vmem,
        scratch_shapes=[pltpu.VMEM(s, d) for s, d in buffers]
        + [pltpu.SemaphoreType.DMA(s) if s else pltpu.SemaphoreType.DMA for s in sems],
        compiler_params=pltpu.CompilerParams(
            collective_id=0, has_side_effects=True, vmem_limit_bytes=56 * 2**20),
    )(row_counts, signals[0], targets[0], feature_weights, spread_ids[None, :], phases[None, :])
    return out[None]


def solution(mesh):
    def run(signals, targets, row_counts, feature_weights, phases, spread_ids):
        fits = plan(
            mesh.shape["epoch"], mesh.shape["asset"], signals.shape[1],
            signals.shape[2], feature_weights.shape[1], targets.shape[2])
        body = fused if fits else on_device
        return body(signals, targets, row_counts, feature_weights, phases, spread_ids)

    placed = (
        P(("grp", "epoch"), "asset", None),
        P(("grp", "epoch"), "asset", None),
        P(("grp", "epoch"), "asset"),
        P(),
        P(),
        P(),
    )
    return jax.shard_map(
        run,
        mesh=mesh,
        in_specs=placed,
        out_specs=P(("grp", "epoch"), "asset", None),
        check_vma=False,
    )
```

```python
import functools
import math

import jax
import jax.numpy as jnp
from jax import lax
from jax.experimental import pallas as pl
from jax.experimental.pallas import tpu as pltpu
from jax.sharding import PartitionSpec as P

ITERS = 3


ridge_penalty = 0.05
epsilon = 1e-06


def prefix(part, axis, combine, identity):
    place = lax.axis_index(axis)
    gathered = jax.tree.map(lambda a: lax.all_gather(a, axis), part)
    state = jax.tree.map(lambda a, e: jnp.zeros_like(a) + jnp.asarray(e, a.dtype), part, identity)

    def one(hop, state):
        return combine(
            state, jax.tree.map(lambda a: lax.dynamic_index_in_dim(a, hop, 0, False), gathered)
        )

    return lax.fori_loop(0, place, one, state)


def feature_scale(spread_ids):
    return (
        0.5
        * (
            1.0
            + jnp.where(spread_ids >= 1, 1.0, 0.0)
            + jnp.where(spread_ids >= 2, 2.0, 0.0)
            + jnp.where(spread_ids >= 3, 4.0, 0.0)
        )
    ).astype(jnp.float32)


def make_features(inputs, feature_weights, phases, spread_ids):
    projected = jnp.dot(inputs, feature_weights, preferred_element_type=jnp.float32)
    return jnp.sin(projected * feature_scale(spread_ids) + phases)


def add_pair(earlier, later):
    return (earlier[0] + later[0], earlier[1] + later[1])


def on_device(signals, targets, row_counts, feature_weights, phases, spread_ids):
    rows = signals.shape[1]
    width = feature_weights.shape[1]
    tgt_width = targets.shape[2]
    groups = lax.axis_size("asset")
    block_size = width // groups
    entries = width * tgt_width
    own_rows = row_counts[0, 0]
    all_counts = lax.all_gather(row_counts[0], "asset", axis=0, tiled=True)
    row_sum = jnp.sum(all_counts).astype(jnp.float32)
    inputs = signals[0]
    returns = targets[0]
    features = make_features(inputs, feature_weights, phases, spread_ids)
    live_mask = (jnp.arange(rows) < own_rows)[:, None]
    features = jnp.where(live_mask, features, jnp.zeros_like(features))
    returns = jnp.where(live_mask, returns.astype(jnp.float32), jnp.zeros((), jnp.float32))
    combined = jnp.concatenate([features, returns], axis=1)
    contract_rows = (((0,), (0,)), ((), ()))
    gram_block = lax.psum_scatter(
        lax.dot_general(features, combined, contract_rows, precision=lax.Precision.HIGHEST),
        "asset",
        scatter_dimension=0,
        tiled=True,
    )
    earlier, earlier_rows = prefix(
        (gram_block, row_sum),
        "epoch",
        add_pair,
        (jnp.zeros_like(gram_block), jnp.zeros((), jnp.float32)),
    )
    cumulative = earlier + gram_block
    row_total = earlier_rows + row_sum
    first_row = lax.axis_index("asset") * block_size
    diagonal = jnp.arange(width)[None, :] == first_row + jnp.arange(block_size)[:, None]
    system = cumulative[:, :width] / row_total + ridge_penalty * jnp.where(
        diagonal, 1.0, 0.0
    ).astype(jnp.float32)
    residual = cumulative[:, width:] / row_total
    coef = jnp.zeros((block_size, tgt_width), jnp.float32)
    for iteration in range(ITERS):
        image = jnp.zeros((block_size, tgt_width), jnp.float32) + jnp.dot(
            system,
            lax.all_gather(residual, "asset", axis=0, tiled=True),
            precision=lax.Precision.HIGHEST,
        )
        res_norm, res_curve = lax.psum(
            (jnp.sum(residual * residual), jnp.sum(residual * image)), "asset"
        )
        step_size = res_norm / entries / (res_curve / entries + epsilon)
        coef = coef + step_size * residual
        residual = residual - step_size * image
    return (jnp.sqrt(row_total) * coef)[None]


MESH = pl.DeviceIdType.MESH
MASK_ROWS = 16
COS = (
    0.9999992251396179,
    -19.738977432250977,
    64.9285888671875,
    -85.27084350585938,
    58.78694152832031,
    -21.0654296875,
)
ROUNDER = 1.5 * 2.0**23
def mm(a, b):
    return jnp.dot(a, b, preferred_element_type=jnp.float32)


def split(a):
    high = a.astype(jnp.bfloat16)
    return high, (a - high.astype(jnp.float32)).astype(jnp.bfloat16)


def kernel(
    X, Z, chunk, entries,
    counts_ref, sig_ref, y_ref, w_ref, ids_ref, phases_ref, out_ref,
    yt_own, sc_ref, ph_ref,
    sig_all, yt_all, hi, lo, proj, lhs, msk, vec, coef, vs, ust, own, got, totals, got_totals,
    scal, last, outbox, landing,
    gs_send, gs_recv, gy_send, gy_recv, fs_send, fs_recv, fy_send, fy_recv,
    ex_send, ex_recv, t_send, t_recv,
    sc_send, sc_recv, la_send, la_recv, o_send, o_recv,
):
    rows, K = sig_ref.shape
    F = w_ref.shape[1]
    cols = y_ref.shape[1] // Z
    C = 2 * cols
    B = X * Z
    n = B * rows
    nch = F // chunk
    band = 2 * rows
    f32 = jnp.float32
    epoch = lax.axis_index("epoch")
    z = lax.axis_index("asset")
    x = epoch // 2
    core = epoch % 2

    def at(xx, cc, zz):
        return {"epoch": 2 * xx + cc, "asset": zz}

    def signal(peer):
        pl.semaphore_signal(barrier, inc=1, device_id=peer, device_id_type=MESH)

    barrier = pltpu.get_barrier_semaphore()
    for d in range(1, Z):
        signal(at(x, core, lax.rem(z + d, Z)))
    for d in range(Z):
        signal(at(x, 1 - core, lax.rem(z + d, Z)))

    beside = sorted({1 % X, X - 1} - {0})
    for d in beside:
        signal(at(lax.rem(x + d, X), core, z))

    count_here = counts_ref[0, 0]
    alive = lax.broadcasted_iota(jnp.int32, (rows, 1), 0) < count_here
    y = jnp.where(alive, y_ref[...].astype(f32), 0.0).T
    alive = lax.broadcasted_iota(jnp.int32, (MASK_ROWS, rows), 1) < count_here
    mask = jnp.where(alive, 1.0, 0.0).astype(jnp.bfloat16)
    for b in range(Z):
        yt_own[b, 0:cols, :] = y[b * cols:(b + 1) * cols].astype(jnp.bfloat16)
        yt_own[b, cols:cols + MASK_ROWS, :] = mask
    turn = 1.0 / (2.0 * math.pi)
    sc_ref[...] = feature_scale(ids_ref[...]) * turn
    ph_ref[...] = phases_ref[...] * turn - 0.25

    pl.semaphore_wait(barrier, 2 * Z - 1 + len(beside))

    mine = x * Z + z

    def along(d):
        zz = lax.rem(z + d, Z)
        return (
            pltpu.make_async_remote_copy(
                src_ref=sig_ref, dst_ref=sig_all.at[mine],
                send_sem=gs_send.at[d], recv_sem=gs_recv.at[d],
                device_id=at(x, core, zz), device_id_type=MESH),
            pltpu.make_async_remote_copy(
                src_ref=yt_own.at[zz], dst_ref=yt_all.at[mine],
                send_sem=gy_send.at[d], recv_sem=gy_recv.at[d],
                device_id=at(x, core, zz), device_id_type=MESH),
        )

    def upward(slot):
        return (
            pltpu.make_async_remote_copy(
                src_ref=sig_all.at[slot], dst_ref=sig_all.at[slot],
                send_sem=fs_send.at[slot], recv_sem=fs_recv.at[slot],
                device_id=at(x + 1, core, z), device_id_type=MESH),
            pltpu.make_async_remote_copy(
                src_ref=yt_all.at[slot], dst_ref=yt_all.at[slot],
                send_sem=fy_send.at[slot], recv_sem=fy_recv.at[slot],
                device_id=at(x + 1, core, z), device_id_type=MESH),
        )

    for d in range(1, Z):
        for copy in along(d):
            copy.start()
    sig_all[mine] = sig_ref[...]
    yt_all[mine] = yt_own[z]

    def block(dz, dx):
        xx = x - dx
        zz = lax.rem(z + Z - dz, Z)
        slot = xx * Z + zz

        @pl.when((dx == 0) & (dz > 0))
        def _():
            for copy in along(dz):
                copy.wait()

        @pl.when(dx > 0)
        def _():
            for copy in upward(slot):
                copy.wait_recv()

        @pl.when(x < X - 1)
        def _():
            for copy in upward(slot):
                copy.start()

        base = pl.multiple_of(slot * rows, rows)
        live = yt_all[slot, cols:cols + MASK_ROWS, :].astype(f32)[0:1, :]
        y = yt_all[slot, 0:cols, :].astype(f32)
        for q in range(2):
            allow = jnp.where(2 * xx + core <= 2 * x + q, 1.0, 0.0).astype(f32)
            msk[q, :, pl.ds(base, rows)] = jnp.broadcast_to(live * allow, (8, rows))
            lhs[q * cols:(q + 1) * cols, :] = (y * allow).astype(jnp.bfloat16)
        for k in range(nch):
            part = slice(k * chunk, (k + 1) * chunk)
            proj[:, part] = mm(sig_all[slot], w_ref[:, part])
        for k in range(nch):
            part = slice(k * chunk, (k + 1) * chunk)
            scale = sc_ref[:, part]
            phase = ph_ref[:, part]

            def strip(r, carry):
                r0 = pl.multiple_of(r * 16, 16)
                t = proj[pl.ds(r0, 16), part] * scale + phase
                f = t - ((t + ROUNDER) - ROUNDER)
                s = f * f
                acc = s * COS[-1] + COS[-2]
                for c in COS[-3::-1]:
                    acc = acc * s + c
                high, low = split(acc)
                to = pl.ds(pl.multiple_of(base + r0, 16), 16)
                hi[to, part] = high
                lo[to, part] = low
                return carry

            lax.fori_loop(0, rows // 16, strip, 0, unroll=4)
            here = pl.ds(base, rows)
            vec[:, part] += mm(lhs[...], hi[here, part]) + mm(lhs[...], lo[here, part])

    vec[...] = jnp.zeros_like(vec)

    def column(dz, carry):
        def one(dx, carry):
            block(dz, dx)
            return carry

        return lax.fori_loop(0, x + 1, one, carry)

    lax.fori_loop(0, Z, column, 0)

    def absent(slot, carry):
        here = pl.ds(pl.multiple_of(slot * rows, rows), rows)
        hi[here, :] = jnp.zeros((rows, F), jnp.bfloat16)
        lo[here, :] = jnp.zeros((rows, F), jnp.bfloat16)
        msk[:, :, here] = jnp.zeros((2, 8, rows), f32)
        return carry

    lax.fori_loop((x + 1) * Z, B, absent, 0)

    @pl.when(x < X - 1)
    def _():
        def sent(slot, carry):
            for copy in upward(slot):
                copy.wait_send()
            return carry

        lax.fori_loop(0, (x + 1) * Z, sent, 0)

    is_first = lax.broadcasted_iota(jnp.int32, (C, 1), 0) < cols

    def spread(a0, a1):
        return jnp.where(is_first, a0, a1)

    totals[...] = jnp.zeros_like(totals)
    for q in range(2):
        totals[q] = jnp.broadcast_to(jnp.sum(msk[q], axis=1, keepdims=True), totals.shape[1:])
    count_copy = pltpu.make_async_remote_copy(
        src_ref=totals, dst_ref=got_totals, send_sem=t_send, recv_sem=t_recv,
        device_id=at(x, 1 - core, z), device_id_type=MESH)
    count_copy.start()

    def exchange(s, k):
        return pltpu.make_async_remote_copy(
            src_ref=own.at[s, k], dst_ref=got.at[s, k],
            send_sem=ex_send.at[s, k], recv_sem=ex_recv.at[s, k],
            device_id=at(x, 1 - core, z), device_id_type=MESH)

    for k in range(nch):
        part = slice(k * chunk, (k + 1) * chunk)
        own[0, k] = vec[:, part]
        exchange(0, k).start()
    count_copy.wait()
    count = [totals[q][0:1, 0:1] + got_totals[q][0:1, 0:1] for q in range(2)]
    inverse = spread(1.0 / count[0], 1.0 / count[1])

    def keep(v, part):
        high, low = split(v.T)
        vs[part, 0:C] = high
        vs[part, C:2 * C] = low

    norm = jnp.zeros((C, 1), f32)
    for k in range(nch):
        part = slice(k * chunk, (k + 1) * chunk)
        exchange(0, k).wait()
        v = (own[0, k] + got[0, k]) * inverse
        vec[:, part] = v
        keep(v, part)
        norm = norm + jnp.sum(v * v, axis=1, keepdims=True)

    tile_row = lax.broadcasted_iota(jnp.int32, (8, 128), 0)

    def tile(norm, curve):
        out = jnp.zeros((8, 128), f32)
        for i, a in enumerate((norm[0:cols], norm[cols:], curve[0:cols], curve[cols:])):
            out = jnp.where(tile_row == i, jnp.sum(a, axis=0, keepdims=True), out)
        return out

    def step_of(a):
        res_norm = spread(a[0:1, 0:1], a[1:2, 0:1])
        res_curve = spread(a[2:3, 0:1], a[3:4, 0:1])
        return res_norm / entries / (res_curve / entries + epsilon)

    for it in range(ITERS):
        final = it == ITERS - 1

        def forward(j, total):
            base = pl.multiple_of(j * band, band)
            here = pl.ds(base, band)
            if final:
                u = mm(hi[here, :], vs[:, 0:C]).T
            else:
                u = mm(hi[here, :], vs[...])
                u = (u[:, 0:C] + u[:, C:]).T
            u = jnp.concatenate(
                [u[0:cols] * msk[0, 0:1, here], u[cols:] * msk[1, 0:1, here]], axis=0)
            if final:
                return total + jnp.sum(u * u, axis=1, keepdims=True)
            high, low = split(u)
            ust[0:C, here] = high
            ust[C:2 * C, here] = low
            return total

        square = lax.fori_loop(0, n // band, forward, jnp.zeros((C, 1), f32))
        if final:
            last[core * Z + z] = tile(norm, square)
            copies = []
            for d in range(1, 2 * Z):
                cc, zz = lax.rem(core + d // Z, 2), lax.rem(z + d % Z, Z)
                copies.append(pltpu.make_async_remote_copy(
                    src_ref=last.at[core * Z + z], dst_ref=last.at[core * Z + z],
                    send_sem=la_send.at[d], recv_sem=la_recv.at[d],
                    device_id=at(x, cc, zz), device_id_type=MESH))
            for copy in copies:
                copy.start()
            for copy in copies:
                copy.wait()
            a = last[0]
            for i in range(1, 2 * Z):
                a = a + last[i]
            norms = spread(a[0:1, 0:1], a[1:2, 0:1]) * 0.5
            curve = spread(a[2:3, 0:1] / count[0], a[3:4, 0:1] / count[1]) + ridge_penalty * norms
            step = norms / entries / (curve / entries + epsilon)
            root = spread(jnp.sqrt(count[0]), jnp.sqrt(count[1]))
            for k in range(nch):
                part = slice(k * chunk, (k + 1) * chunk)
                coef[:, part] = (coef[:, part] + step * vec[:, part]) * root
        else:
            s = it + 1
            for k in range(nch):
                part = slice(k * chunk, (k + 1) * chunk)
                image = mm(ust[...], hi[:, part])
                own[s, k] = image[0:C] + image[C:] + mm(ust[0:C, :], lo[:, part])
                exchange(s, k).start()
            curve = jnp.zeros((C, 1), f32)
            for k in range(nch):
                part = slice(k * chunk, (k + 1) * chunk)
                exchange(s, k).wait()
                v = vec[:, part]
                image = (own[s, k] + got[s, k]) * inverse + ridge_penalty * v
                proj[0:C, part] = image
                curve = curve + jnp.sum(v * image, axis=1, keepdims=True)
            scal[it, z] = tile(norm, curve)
            copies = []
            for d in range(1, Z):
                copies.append(pltpu.make_async_remote_copy(
                    src_ref=scal.at[it, z], dst_ref=scal.at[it, z],
                    send_sem=sc_send.at[it, d], recv_sem=sc_recv.at[it, d],
                    device_id=at(x, core, lax.rem(z + d, Z)), device_id_type=MESH))
            for copy in copies:
                copy.start()
            for copy in copies:
                copy.wait()
            a = scal[it, 0]
            for i in range(1, Z):
                a = a + scal[it, i]
            step = step_of(a)
            norm = jnp.zeros((C, 1), f32)
            for k in range(nch):
                part = slice(k * chunk, (k + 1) * chunk)
                v = vec[:, part]
                coef[:, part] = step * v if it == 0 else coef[:, part] + step * v
                v = v - step * proj[0:C, part]
                vec[:, part] = v
                keep(v, part)
                norm = norm + jnp.sum(v * v, axis=1, keepdims=True)

    width = F // Z
    first = pl.multiple_of(core * cols, cols)
    for b in range(Z):
        outbox[b] = coef[pl.ds(first, cols), b * width:(b + 1) * width]
    copies = []
    for d in range(1, Z):
        zz = lax.rem(z + d, Z)
        copies.append(pltpu.make_async_remote_copy(
            src_ref=outbox.at[zz], dst_ref=landing.at[z],
            send_sem=o_send.at[d], recv_sem=o_recv.at[d],
            device_id=at(x, core, zz), device_id_type=MESH))
    for copy in copies:
        copy.start()
    landing[z] = outbox[z]
    for copy in copies:
        copy.wait()
    out_ref[...] = landing[...].reshape(Z * cols, width).T


def scratch_of(X, Z, rows, K, F, cols, chunk):
    B = X * Z
    n = B * rows
    C = 2 * cols
    nch = F // chunk
    f32, bf16 = jnp.float32, jnp.bfloat16
    buffers = [
        ((Z, cols + MASK_ROWS, rows), bf16), ((1, F), f32), ((1, F), f32),
        ((B, rows, K), bf16), ((B, cols + MASK_ROWS, rows), bf16),
        ((n, F), bf16), ((n, F), bf16), ((max(rows, C), F), f32), ((C, rows), bf16),
        ((2, 8, n), f32), ((C, F), f32), ((C, F), f32), ((F, 2 * C), bf16), ((2 * C, n), bf16),
        ((ITERS, nch, C, chunk), f32), ((ITERS, nch, C, chunk), f32),
        ((2, 8, 128), f32), ((2, 8, 128), f32),
        ((ITERS, Z, 8, 128), f32), ((2 * Z, 8, 128), f32),
        ((Z, cols, F // Z), f32), ((Z, cols, F // Z), f32),
    ]
    held = sum(math.prod(shape) * jnp.dtype(dtype).itemsize for shape, dtype in buffers)
    sems = [(Z,)] * 4 + [(B,)] * 4 + [(ITERS, nch)] * 2 + [()] * 2 + [(ITERS, Z)] * 2 + [(2 * Z,)] * 2 + [(Z,)] * 2
    return buffers, sems, held


VMEM_BUDGET = 44 * 2**20


def plan(E, Z, rows, K, F, T):
    if E % 2 or T % Z or F % Z:
        return None
    cols, chunk = T // Z, 512
    if (E // 2 * Z) % 2 or cols % 16 or rows % 128 or F % chunk or (F // Z) % 128 or K % 128:
        return None
    buffers, sems, held = scratch_of(E // 2, Z, rows, K, F, cols, chunk)
    if held > VMEM_BUDGET:
        return None
    return cols, chunk, buffers, sems


def fused(signals, targets, row_counts, feature_weights, phases, spread_ids):
    E, Z = lax.axis_size("epoch"), lax.axis_size("asset")
    rows, K = signals.shape[1:]
    F = feature_weights.shape[1]
    T = targets.shape[2]
    cols, chunk, buffers, sems = plan(E, Z, rows, K, F, T)
    vmem = pl.BlockSpec(memory_space=pltpu.VMEM)
    out = pl.pallas_call(
        functools.partial(kernel, E // 2, Z, chunk, float(F * T)),
        out_shape=jax.ShapeDtypeStruct((F // Z, T), jnp.float32),
        in_specs=[pl.BlockSpec(memory_space=pltpu.SMEM)] + [vmem] * 5,
        out_specs=vmem,
        scratch_shapes=[pltpu.VMEM(s, d) for s, d in buffers]
        + [pltpu.SemaphoreType.DMA(s) if s else pltpu.SemaphoreType.DMA for s in sems],
        compiler_params=pltpu.CompilerParams(
            collective_id=0, has_side_effects=True, vmem_limit_bytes=56 * 2**20),
    )(row_counts, signals[0], targets[0], feature_weights, spread_ids[None, :], phases[None, :])
    return out[None]


def solution(mesh):
    def run(signals, targets, row_counts, feature_weights, phases, spread_ids):
        fits = plan(
            mesh.shape["epoch"], mesh.shape["asset"], signals.shape[1],
            signals.shape[2], feature_weights.shape[1], targets.shape[2])
        body = fused if fits else on_device
        return body(signals, targets, row_counts, feature_weights, phases, spread_ids)

    placed = (
        P(("grp", "epoch"), "asset", None),
        P(("grp", "epoch"), "asset", None),
        P(("grp", "epoch"), "asset"),
        P(),
        P(),
        P(),
    )
    return jax.shard_map(
        run,
        mesh=mesh,
        in_specs=placed,
        out_specs=P(("grp", "epoch"), "asset", None),
        check_vma=False,
    )
```

```python
import functools
import math

import jax
import jax.numpy as jnp
from jax import lax
from jax.experimental import pallas as pl
from jax.experimental.pallas import tpu as pltpu
from jax.sharding import PartitionSpec as P

ITERS = 3


ridge_penalty = 0.05
epsilon = 1e-06


def prefix(part, axis, combine, identity):
    place = lax.axis_index(axis)
    gathered = jax.tree.map(lambda a: lax.all_gather(a, axis), part)
    state = jax.tree.map(lambda a, e: jnp.zeros_like(a) + jnp.asarray(e, a.dtype), part, identity)

    def one(hop, state):
        return combine(
            state, jax.tree.map(lambda a: lax.dynamic_index_in_dim(a, hop, 0, False), gathered)
        )

    return lax.fori_loop(0, place, one, state)


def feature_scale(spread_ids):
    return (
        0.5
        * (
            1.0
            + jnp.where(spread_ids >= 1, 1.0, 0.0)
            + jnp.where(spread_ids >= 2, 2.0, 0.0)
            + jnp.where(spread_ids >= 3, 4.0, 0.0)
        )
    ).astype(jnp.float32)


def make_features(inputs, feature_weights, phases, spread_ids):
    projected = jnp.dot(inputs, feature_weights, preferred_element_type=jnp.float32)
    return jnp.sin(projected * feature_scale(spread_ids) + phases)


def add_pair(earlier, later):
    return (earlier[0] + later[0], earlier[1] + later[1])


def on_device(signals, targets, row_counts, feature_weights, phases, spread_ids):
    rows = signals.shape[1]
    width = feature_weights.shape[1]
    tgt_width = targets.shape[2]
    groups = lax.axis_size("asset")
    block_size = width // groups
    entries = width * tgt_width
    own_rows = row_counts[0, 0]
    all_counts = lax.all_gather(row_counts[0], "asset", axis=0, tiled=True)
    row_sum = jnp.sum(all_counts).astype(jnp.float32)
    inputs = signals[0]
    returns = targets[0]
    features = make_features(inputs, feature_weights, phases, spread_ids)
    live_mask = (jnp.arange(rows) < own_rows)[:, None]
    features = jnp.where(live_mask, features, jnp.zeros_like(features))
    returns = jnp.where(live_mask, returns.astype(jnp.float32), jnp.zeros((), jnp.float32))
    combined = jnp.concatenate([features, returns], axis=1)
    contract_rows = (((0,), (0,)), ((), ()))
    gram_block = lax.psum_scatter(
        lax.dot_general(features, combined, contract_rows, precision=lax.Precision.HIGHEST),
        "asset",
        scatter_dimension=0,
        tiled=True,
    )
    earlier, earlier_rows = prefix(
        (gram_block, row_sum),
        "epoch",
        add_pair,
        (jnp.zeros_like(gram_block), jnp.zeros((), jnp.float32)),
    )
    cumulative = earlier + gram_block
    row_total = earlier_rows + row_sum
    first_row = lax.axis_index("asset") * block_size
    diagonal = jnp.arange(width)[None, :] == first_row + jnp.arange(block_size)[:, None]
    system = cumulative[:, :width] / row_total + ridge_penalty * jnp.where(
        diagonal, 1.0, 0.0
    ).astype(jnp.float32)
    residual = cumulative[:, width:] / row_total
    coef = jnp.zeros((block_size, tgt_width), jnp.float32)
    for iteration in range(ITERS):
        image = jnp.zeros((block_size, tgt_width), jnp.float32) + jnp.dot(
            system,
            lax.all_gather(residual, "asset", axis=0, tiled=True),
            precision=lax.Precision.HIGHEST,
        )
        res_norm, res_curve = lax.psum(
            (jnp.sum(residual * residual), jnp.sum(residual * image)), "asset"
        )
        step_size = res_norm / entries / (res_curve / entries + epsilon)
        coef = coef + step_size * residual
        residual = residual - step_size * image
    return (jnp.sqrt(row_total) * coef)[None]


MESH = pl.DeviceIdType.MESH
MASK_ROWS = 16
COS = (
    0.9999992251396179,
    -19.738977432250977,
    64.9285888671875,
    -85.27084350585938,
    58.78694152832031,
    -21.0654296875,
)
ROUNDER = 1.5 * 2.0**23
def mm(a, b):
    return jnp.dot(a, b, preferred_element_type=jnp.float32)


def split(a):
    high = a.astype(jnp.bfloat16)
    return high, (a - high.astype(jnp.float32)).astype(jnp.bfloat16)


def kernel(
    X, Z, chunk, entries,
    counts_ref, sig_ref, y_ref, w_ref, ids_ref, phases_ref, out_ref,
    yt_own, sc_ref, ph_ref,
    sig_all, yt_all, hi, lo, proj, lhs, msk, vec, res, u_now, u_image, vs, ust, own, got, totals, got_totals,
    scal, last, outbox, landing,
    gs_send, gs_recv, gy_send, gy_recv, fs_send, fs_recv, fy_send, fy_recv,
    ex_send, ex_recv, t_send, t_recv,
    sc_send, sc_recv, la_send, la_recv, o_send, o_recv,
):
    rows, K = sig_ref.shape
    F = w_ref.shape[1]
    cols = y_ref.shape[1] // Z
    C = 2 * cols
    B = X * Z
    n = B * rows
    nch = F // chunk
    band = 2 * rows
    f32 = jnp.float32
    epoch = lax.axis_index("epoch")
    z = lax.axis_index("asset")
    x = epoch // 2
    core = epoch % 2

    def at(xx, cc, zz):
        return {"epoch": 2 * xx + cc, "asset": zz}

    def signal(peer):
        pl.semaphore_signal(barrier, inc=1, device_id=peer, device_id_type=MESH)

    barrier = pltpu.get_barrier_semaphore()
    for d in range(1, Z):
        signal(at(x, core, lax.rem(z + d, Z)))
    for d in range(Z):
        signal(at(x, 1 - core, lax.rem(z + d, Z)))

    beside = sorted({1 % X, X - 1} - {0})
    for d in beside:
        signal(at(lax.rem(x + d, X), core, z))

    count_here = counts_ref[0, 0]
    alive = lax.broadcasted_iota(jnp.int32, (rows, 1), 0) < count_here
    y = jnp.where(alive, y_ref[...].astype(f32), 0.0).T
    alive = lax.broadcasted_iota(jnp.int32, (MASK_ROWS, rows), 1) < count_here
    mask = jnp.where(alive, 1.0, 0.0).astype(jnp.bfloat16)
    for b in range(Z):
        yt_own[b, 0:cols, :] = y[b * cols:(b + 1) * cols].astype(jnp.bfloat16)
        yt_own[b, cols:cols + MASK_ROWS, :] = mask
    turn = 1.0 / (2.0 * math.pi)
    sc_ref[...] = feature_scale(ids_ref[...]) * turn
    ph_ref[...] = phases_ref[...] * turn - 0.25

    pl.semaphore_wait(barrier, 2 * Z - 1 + len(beside))

    mine = x * Z + z

    def along(d):
        zz = lax.rem(z + d, Z)
        return (
            pltpu.make_async_remote_copy(
                src_ref=sig_ref, dst_ref=sig_all.at[mine],
                send_sem=gs_send.at[d], recv_sem=gs_recv.at[d],
                device_id=at(x, core, zz), device_id_type=MESH),
            pltpu.make_async_remote_copy(
                src_ref=yt_own.at[zz], dst_ref=yt_all.at[mine],
                send_sem=gy_send.at[d], recv_sem=gy_recv.at[d],
                device_id=at(x, core, zz), device_id_type=MESH),
        )

    def upward(slot):
        return (
            pltpu.make_async_remote_copy(
                src_ref=sig_all.at[slot], dst_ref=sig_all.at[slot],
                send_sem=fs_send.at[slot], recv_sem=fs_recv.at[slot],
                device_id=at(x + 1, core, z), device_id_type=MESH),
            pltpu.make_async_remote_copy(
                src_ref=yt_all.at[slot], dst_ref=yt_all.at[slot],
                send_sem=fy_send.at[slot], recv_sem=fy_recv.at[slot],
                device_id=at(x + 1, core, z), device_id_type=MESH),
        )

    for d in range(1, Z):
        for copy in along(d):
            copy.start()
    sig_all[mine] = sig_ref[...]
    yt_all[mine] = yt_own[z]

    is_first = lax.broadcasted_iota(jnp.int32, (C, 1), 0) < cols

    def spread(a0, a1):
        return jnp.where(is_first, a0, a1)

    def exchange(s, k):
        return pltpu.make_async_remote_copy(
            src_ref=own.at[s, k], dst_ref=got.at[s, k],
            send_sem=ex_send.at[s, k], recv_sem=ex_recv.at[s, k],
            device_id=at(x, 1 - core, z), device_id_type=MESH)

    def block(dz, dx):
        xx = x - dx
        zz = lax.rem(z + Z - dz, Z)
        slot = xx * Z + zz

        @pl.when((dx == 0) & (dz > 0))
        def _():
            for copy in along(dz):
                copy.wait()

        @pl.when(dx > 0)
        def _():
            for copy in upward(slot):
                copy.wait_recv()

        @pl.when(x < X - 1)
        def _():
            for copy in upward(slot):
                copy.start()

        base = pl.multiple_of(slot * rows, rows)
        live = yt_all[slot, cols:cols + MASK_ROWS, :].astype(f32)[0:1, :]
        y = yt_all[slot, 0:cols, :].astype(f32)
        for q in range(2):
            allow = jnp.where(2 * xx + core <= 2 * x + q, 1.0, 0.0).astype(f32)
            msk[q, :, pl.ds(base, rows)] = jnp.broadcast_to(live * allow, (8, rows))
            lhs[q * cols:(q + 1) * cols, :] = (y * allow).astype(jnp.bfloat16)
        for k in range(nch):
            part = slice(k * chunk, (k + 1) * chunk)
            proj[:, part] = mm(sig_all[slot], w_ref[:, part])
        for k in range(nch):
            part = slice(k * chunk, (k + 1) * chunk)
            scale = sc_ref[:, part]
            phase = ph_ref[:, part]

            def strip(r, carry):
                r0 = pl.multiple_of(r * 16, 16)
                t = proj[pl.ds(r0, 16), part] * scale + phase
                f = t - ((t + ROUNDER) - ROUNDER)
                s = f * f
                acc = s * COS[-1] + COS[-2]
                for c in COS[-3::-1]:
                    acc = acc * s + c
                high, low = split(acc)
                to = pl.ds(pl.multiple_of(base + r0, 16), 16)
                hi[to, part] = high
                lo[to, part] = low
                return carry

            lax.fori_loop(0, rows // 16, strip, 0, unroll=4)
            here = pl.ds(base, rows)
            own[0, k] += mm(lhs[...], hi[here, part]) + mm(lhs[...], lo[here, part])

            @pl.when((dz == Z - 1) & (dx == x))
            def _():
                exchange(0, k).start()

    own[0] = jnp.zeros((nch, C, chunk), f32)

    def column(dz, carry):
        def one(dx, carry):
            block(dz, dx)
            return carry

        return lax.fori_loop(0, x + 1, one, carry)

    lax.fori_loop(0, Z, column, 0)

    def absent(slot, carry):
        here = pl.ds(pl.multiple_of(slot * rows, rows), rows)
        hi[here, :] = jnp.zeros((rows, F), jnp.bfloat16)
        lo[here, :] = jnp.zeros((rows, F), jnp.bfloat16)
        msk[:, :, here] = jnp.zeros((2, 8, rows), f32)
        return carry

    lax.fori_loop((x + 1) * Z, B, absent, 0)

    @pl.when(x < X - 1)
    def _():
        def sent(slot, carry):
            for copy in upward(slot):
                copy.wait_send()
            return carry

        lax.fori_loop(0, (x + 1) * Z, sent, 0)

    for q in range(2):
        totals[q] = jnp.broadcast_to(jnp.sum(msk[q], axis=1, keepdims=True), totals.shape[1:])
    count_copy = pltpu.make_async_remote_copy(
        src_ref=totals, dst_ref=got_totals, send_sem=t_send, recv_sem=t_recv,
        device_id=at(x, 1 - core, z), device_id_type=MESH)
    count_copy.start()
    count_copy.wait()
    count = [totals[q][0:1, 0:1] + got_totals[q][0:1, 0:1] for q in range(2)]
    inverse = spread(1.0 / count[0], 1.0 / count[1])

    width = F // Z
    first = pl.multiple_of(core * cols, cols)

    def piece(s, d):
        zz = lax.rem(z + d, Z)
        columns = pl.ds(pl.multiple_of(zz * width, width), width)
        return pltpu.make_async_remote_copy(
            src_ref=vec.at[s, pl.ds(first, cols), columns], dst_ref=landing.at[s, z],
            send_sem=o_send.at[s, d], recv_sem=o_recv.at[s, d],
            device_id=at(x, core, zz), device_id_type=MESH)

    def send_pieces(s):
        for d in range(1, Z):
            piece(s, d).start()
        columns = pl.ds(pl.multiple_of(z * width, width), width)
        landing[s, z] = vec[s, pl.ds(first, cols), columns]

    def keep(v, part):
        high, low = split(v.T)
        vs[part, 0:C] = high
        vs[part, C:2 * C] = low

    def forward(to):
        def one(j, carry):
            here = pl.ds(pl.multiple_of(j * band, band), band)
            u = mm(hi[here, :], vs[...])
            u = (u[:, 0:C] + u[:, C:]).T
            to[0:cols, here] = u[0:cols] * msk[0, 0:1, here]
            to[cols:C, here] = u[cols:] * msk[1, 0:1, here]
            return carry

        lax.fori_loop(0, n // band, one, 0)

    norm = jnp.zeros((C, 1), f32)
    for k in range(nch):
        part = slice(k * chunk, (k + 1) * chunk)
        exchange(0, k).wait()
        v = (own[0, k] + got[0, k]) * inverse
        vec[0, :, part] = v
        keep(v, part)
        norm = norm + jnp.sum(v * v, axis=1, keepdims=True)
    send_pieces(0)
    forward(u_now)

    tile_row = lax.broadcasted_iota(jnp.int32, (8, 128), 0)

    def tile(norm, curve):
        out = jnp.zeros((8, 128), f32)
        for i, a in enumerate((norm[0:cols], norm[cols:], curve[0:cols], curve[cols:])):
            out = jnp.where(tile_row == i, jnp.sum(a, axis=0, keepdims=True), out)
        return out

    steps = []
    for it in range(ITERS - 1):
        s = it + 1
        for k in range(n // chunk):
            part = slice(k * chunk, (k + 1) * chunk)
            high, low = split(u_now[:, part])
            ust[0:C, part] = high
            ust[C:2 * C, part] = low
        for k in range(nch):
            part = slice(k * chunk, (k + 1) * chunk)
            image = mm(ust[...], hi[:, part])
            own[s, k] = image[0:C] + image[C:] + mm(ust[0:C, :], lo[:, part])
            exchange(s, k).start()
        curve = jnp.zeros((C, 1), f32)
        for k in range(nch):
            part = slice(k * chunk, (k + 1) * chunk)
            exchange(s, k).wait()
            v = res[:, part] if it else vec[0, :, part]
            image = (own[s, k] + got[s, k]) * inverse + ridge_penalty * v
            vec[s, :, part] = image
            keep(image, part)
            curve = curve + jnp.sum(v * image, axis=1, keepdims=True)
        scal[it, z] = tile(norm, curve)
        copies = []
        for d in range(1, Z):
            copies.append(pltpu.make_async_remote_copy(
                src_ref=scal.at[it, z], dst_ref=scal.at[it, z],
                send_sem=sc_send.at[it, d], recv_sem=sc_recv.at[it, d],
                device_id=at(x, core, lax.rem(z + d, Z)), device_id_type=MESH))
        for copy in copies:
            copy.start()
        send_pieces(s)
        forward(u_image)
        for copy in copies:
            copy.wait()
        a = scal[it, 0]
        for i in range(1, Z):
            a = a + scal[it, i]
        res_norm = spread(a[0:1, 0:1], a[1:2, 0:1])
        res_curve = spread(a[2:3, 0:1], a[3:4, 0:1])
        step = res_norm / entries / (res_curve / entries + epsilon)
        steps.append(step)
        norm = jnp.zeros((C, 1), f32)
        for k in range(nch):
            part = slice(k * chunk, (k + 1) * chunk)
            v = res[:, part] if it else vec[0, :, part]
            v = v - step * vec[s, :, part]
            res[:, part] = v
            norm = norm + jnp.sum(v * v, axis=1, keepdims=True)
        square = jnp.zeros((C, 1), f32)
        for k in range(n // chunk):
            part = slice(k * chunk, (k + 1) * chunk)
            u = u_now[:, part] - step * u_image[:, part]
            u_now[:, part] = u
            square = square + jnp.sum(u * u, axis=1, keepdims=True)

    last[core * Z + z] = tile(norm, square)
    copies = []
    for d in range(1, 2 * Z):
        cc, zz = lax.rem(core + d // Z, 2), lax.rem(z + d % Z, Z)
        copies.append(pltpu.make_async_remote_copy(
            src_ref=last.at[core * Z + z], dst_ref=last.at[core * Z + z],
            send_sem=la_send.at[d], recv_sem=la_recv.at[d],
            device_id=at(x, cc, zz), device_id_type=MESH))
    for copy in copies:
        copy.start()
    for copy in copies:
        copy.wait()
    a = last[0]
    for i in range(1, 2 * Z):
        a = a + last[i]
    norms = spread(a[0:1, 0:1], a[1:2, 0:1]) * 0.5
    curve = spread(a[2:3, 0:1] / count[0], a[3:4, 0:1] / count[1]) + ridge_penalty * norms
    steps.append(norms / entries / (curve / entries + epsilon))

    def here_of(column):
        return jnp.where(core == 0, column[0:1], column[cols:cols + 1])

    root = here_of(spread(jnp.sqrt(count[0]), jnp.sqrt(count[1])))
    s0, s1, s2 = [here_of(step) for step in steps]
    for s in range(ITERS):
        for d in range(1, Z):
            piece(s, d).wait()
    for i in range(Z):
        coef = (s0 + s1 + s2) * landing[0, i] - (s1 + s2) * s0 * landing[1, i]
        coef = coef - s1 * s2 * landing[2, i]
        outbox[i * cols:(i + 1) * cols, :] = coef * root
    out_ref[...] = outbox[...].T


def scratch_of(X, Z, rows, K, F, cols, chunk):
    B = X * Z
    n = B * rows
    C = 2 * cols
    nch = F // chunk
    f32, bf16 = jnp.float32, jnp.bfloat16
    buffers = [
        ((Z, cols + MASK_ROWS, rows), bf16), ((1, F), f32), ((1, F), f32),
        ((B, rows, K), bf16), ((B, cols + MASK_ROWS, rows), bf16),
        ((n, F), bf16), ((n, F), bf16), ((rows, F), f32), ((C, rows), bf16),
        ((2, 8, n), f32), ((ITERS, C, F), f32), ((C, F), f32),
        ((C, n), f32), ((C, n), f32), ((F, 2 * C), bf16), ((2 * C, n), bf16),
        ((ITERS, nch, C, chunk), f32), ((ITERS, nch, C, chunk), f32),
        ((2, 8, 128), f32), ((2, 8, 128), f32),
        ((ITERS, Z, 8, 128), f32), ((2 * Z, 8, 128), f32),
        ((Z * cols, F // Z), f32), ((ITERS, Z, cols, F // Z), f32),
    ]
    held = sum(math.prod(shape) * jnp.dtype(dtype).itemsize for shape, dtype in buffers)
    sems = [(Z,)] * 4 + [(B,)] * 4 + [(ITERS, nch)] * 2 + [()] * 2 + [(ITERS, Z)] * 2 + [(2 * Z,)] * 2 + [(ITERS, Z)] * 2
    return buffers, sems, held


VMEM_BUDGET = 44 * 2**20


def plan(E, Z, rows, K, F, T):
    if E % 2 or T % Z or F % Z:
        return None
    cols, chunk = T // Z, 512
    n_bad = (E // 2 * Z * rows) % chunk
    if (E // 2 * Z) % 2 or ITERS != 3 or n_bad or cols % 16 or rows % 128 or F % chunk or (F // Z) % 128 or K % 128:
        return None
    buffers, sems, held = scratch_of(E // 2, Z, rows, K, F, cols, chunk)
    if held > VMEM_BUDGET:
        return None
    return cols, chunk, buffers, sems


def fused(signals, targets, row_counts, feature_weights, phases, spread_ids):
    E, Z = lax.axis_size("epoch"), lax.axis_size("asset")
    rows, K = signals.shape[1:]
    F = feature_weights.shape[1]
    T = targets.shape[2]
    cols, chunk, buffers, sems = plan(E, Z, rows, K, F, T)
    vmem = pl.BlockSpec(memory_space=pltpu.VMEM)
    out = pl.pallas_call(
        functools.partial(kernel, E // 2, Z, chunk, float(F * T)),
        out_shape=jax.ShapeDtypeStruct((F // Z, T), jnp.float32),
        in_specs=[pl.BlockSpec(memory_space=pltpu.SMEM)] + [vmem] * 5,
        out_specs=vmem,
        scratch_shapes=[pltpu.VMEM(s, d) for s, d in buffers]
        + [pltpu.SemaphoreType.DMA(s) if s else pltpu.SemaphoreType.DMA for s in sems],
        compiler_params=pltpu.CompilerParams(
            collective_id=0, has_side_effects=True, vmem_limit_bytes=56 * 2**20),
    )(row_counts, signals[0], targets[0], feature_weights, spread_ids[None, :], phases[None, :])
    return out[None]


def solution(mesh):
    def run(signals, targets, row_counts, feature_weights, phases, spread_ids):
        fits = plan(
            mesh.shape["epoch"], mesh.shape["asset"], signals.shape[1],
            signals.shape[2], feature_weights.shape[1], targets.shape[2])
        body = fused if fits else on_device
        return body(signals, targets, row_counts, feature_weights, phases, spread_ids)

    placed = (
        P(("grp", "epoch"), "asset", None),
        P(("grp", "epoch"), "asset", None),
        P(("grp", "epoch"), "asset"),
        P(),
        P(),
        P(),
    )
    return jax.shard_map(
        run,
        mesh=mesh,
        in_specs=placed,
        out_specs=P(("grp", "epoch"), "asset", None),
        check_vma=False,
    )
```

```python
import functools
import math

import jax
import jax.numpy as jnp
from jax import lax
from jax.experimental import pallas as pl
from jax.experimental.pallas import tpu as pltpu
from jax.sharding import PartitionSpec as P

ITERS = 3


ridge_penalty = 0.05
epsilon = 1e-06


def prefix(part, axis, combine, identity):
    place = lax.axis_index(axis)
    gathered = jax.tree.map(lambda a: lax.all_gather(a, axis), part)
    state = jax.tree.map(lambda a, e: jnp.zeros_like(a) + jnp.asarray(e, a.dtype), part, identity)

    def one(hop, state):
        return combine(
            state, jax.tree.map(lambda a: lax.dynamic_index_in_dim(a, hop, 0, False), gathered)
        )

    return lax.fori_loop(0, place, one, state)


def feature_scale(spread_ids):
    return (
        0.5
        * (
            1.0
            + jnp.where(spread_ids >= 1, 1.0, 0.0)
            + jnp.where(spread_ids >= 2, 2.0, 0.0)
            + jnp.where(spread_ids >= 3, 4.0, 0.0)
        )
    ).astype(jnp.float32)


def make_features(inputs, feature_weights, phases, spread_ids):
    projected = jnp.dot(inputs, feature_weights, preferred_element_type=jnp.float32)
    return jnp.sin(projected * feature_scale(spread_ids) + phases)


def add_pair(earlier, later):
    return (earlier[0] + later[0], earlier[1] + later[1])


def on_device(signals, targets, row_counts, feature_weights, phases, spread_ids):
    rows = signals.shape[1]
    width = feature_weights.shape[1]
    tgt_width = targets.shape[2]
    groups = lax.axis_size("asset")
    block_size = width // groups
    entries = width * tgt_width
    own_rows = row_counts[0, 0]
    all_counts = lax.all_gather(row_counts[0], "asset", axis=0, tiled=True)
    row_sum = jnp.sum(all_counts).astype(jnp.float32)
    inputs = signals[0]
    returns = targets[0]
    features = make_features(inputs, feature_weights, phases, spread_ids)
    live_mask = (jnp.arange(rows) < own_rows)[:, None]
    features = jnp.where(live_mask, features, jnp.zeros_like(features))
    returns = jnp.where(live_mask, returns.astype(jnp.float32), jnp.zeros((), jnp.float32))
    combined = jnp.concatenate([features, returns], axis=1)
    contract_rows = (((0,), (0,)), ((), ()))
    gram_block = lax.psum_scatter(
        lax.dot_general(features, combined, contract_rows, precision=lax.Precision.HIGHEST),
        "asset",
        scatter_dimension=0,
        tiled=True,
    )
    earlier, earlier_rows = prefix(
        (gram_block, row_sum),
        "epoch",
        add_pair,
        (jnp.zeros_like(gram_block), jnp.zeros((), jnp.float32)),
    )
    cumulative = earlier + gram_block
    row_total = earlier_rows + row_sum
    first_row = lax.axis_index("asset") * block_size
    diagonal = jnp.arange(width)[None, :] == first_row + jnp.arange(block_size)[:, None]
    system = cumulative[:, :width] / row_total + ridge_penalty * jnp.where(
        diagonal, 1.0, 0.0
    ).astype(jnp.float32)
    residual = cumulative[:, width:] / row_total
    coef = jnp.zeros((block_size, tgt_width), jnp.float32)
    for iteration in range(ITERS):
        image = jnp.zeros((block_size, tgt_width), jnp.float32) + jnp.dot(
            system,
            lax.all_gather(residual, "asset", axis=0, tiled=True),
            precision=lax.Precision.HIGHEST,
        )
        res_norm, res_curve = lax.psum(
            (jnp.sum(residual * residual), jnp.sum(residual * image)), "asset"
        )
        step_size = res_norm / entries / (res_curve / entries + epsilon)
        coef = coef + step_size * residual
        residual = residual - step_size * image
    return (jnp.sqrt(row_total) * coef)[None]


MESH = pl.DeviceIdType.MESH
MASK_ROWS = 16
COS = (
    0.9999992251396179,
    -19.738977432250977,
    64.9285888671875,
    -85.27084350585938,
    58.78694152832031,
    -21.0654296875,
)
ROUNDER = 1.5 * 2.0**23
def mm(a, b):
    return jnp.dot(a, b, preferred_element_type=jnp.float32)


def split(a):
    high = a.astype(jnp.bfloat16)
    return high, (a - high.astype(jnp.float32)).astype(jnp.bfloat16)


def kernel(
    X, Z, chunk, entries,
    counts_ref, sig_ref, y_ref, w_ref, ids_ref, phases_ref, out_ref,
    yt_own, sc_ref, ph_ref,
    sig_all, yt_all, hi, lo, proj, lhs, msk, vec, res, u_now, u_image, vs, ust, own, got, totals, got_totals,
    scal, last, outbox, landing,
    gs_send, gs_recv, gy_send, gy_recv, fs_send, fs_recv, fy_send, fy_recv,
    ex_send, ex_recv, t_send, t_recv,
    sc_send, sc_recv, la_send, la_recv, o_send, o_recv,
):
    rows, K = sig_ref.shape
    F = w_ref.shape[1]
    cols = y_ref.shape[1] // Z
    C = 2 * cols
    B = X * Z
    n = B * rows
    nch = F // chunk
    band = 2 * rows
    f32 = jnp.float32
    epoch = lax.axis_index("epoch")
    z = lax.axis_index("asset")
    x = epoch // 2
    core = epoch % 2

    def at(xx, cc, zz):
        return {"epoch": 2 * xx + cc, "asset": zz}

    def signal(peer):
        pl.semaphore_signal(barrier, inc=1, device_id=peer, device_id_type=MESH)

    barrier = pltpu.get_barrier_semaphore()
    for d in range(1, Z):
        signal(at(x, core, lax.rem(z + d, Z)))
    for d in range(Z):
        signal(at(x, 1 - core, lax.rem(z + d, Z)))

    beside = sorted({1 % X, X - 1} - {0})
    for d in beside:
        signal(at(lax.rem(x + d, X), core, z))

    count_here = counts_ref[0, 0]
    alive = lax.broadcasted_iota(jnp.int32, (rows, 1), 0) < count_here
    y = jnp.where(alive, y_ref[...].astype(f32), 0.0).T
    alive = lax.broadcasted_iota(jnp.int32, (MASK_ROWS, rows), 1) < count_here
    mask = jnp.where(alive, 1.0, 0.0).astype(jnp.bfloat16)
    for b in range(Z):
        yt_own[b, 0:cols, :] = y[b * cols:(b + 1) * cols].astype(jnp.bfloat16)
        yt_own[b, cols:cols + MASK_ROWS, :] = mask
    turn = 1.0 / (2.0 * math.pi)
    sc_ref[...] = feature_scale(ids_ref[...]) * turn
    ph_ref[...] = phases_ref[...] * turn - 0.25

    pl.semaphore_wait(barrier, 2 * Z - 1 + len(beside))

    mine = x * Z + z

    def hop(zz, way):
        slot = x * Z + zz
        return pltpu.make_async_remote_copy(
            src_ref=sig_all.at[slot], dst_ref=sig_all.at[slot],
            send_sem=gs_send.at[way, zz], recv_sem=gs_recv.at[zz],
            device_id=at(x, core, lax.rem(z + 2 * way - 1 + Z, Z)), device_id_type=MESH)

    def y_copy(d):
        zz = lax.rem(z + d, Z)
        return pltpu.make_async_remote_copy(
            src_ref=yt_own.at[zz], dst_ref=yt_all.at[mine],
            send_sem=gy_send.at[d], recv_sem=gy_recv.at[z],
            device_id=at(x, core, zz), device_id_type=MESH)

    def y_arrival(zz):
        return pltpu.make_async_remote_copy(
            src_ref=yt_own.at[zz], dst_ref=yt_all.at[x * Z + zz],
            send_sem=gy_send.at[0], recv_sem=gy_recv.at[zz],
            device_id=at(x, core, zz), device_id_type=MESH)

    def pass_on(zz, act):
        @pl.when((zz <= z) & (z < Z - 1))
        def _():
            act(hop(zz, 1))

        @pl.when((zz >= z) & (z > 0))
        def _():
            act(hop(zz, 0))

    def upward(slot):
        return (
            pltpu.make_async_remote_copy(
                src_ref=sig_all.at[slot], dst_ref=sig_all.at[slot],
                send_sem=fs_send.at[slot], recv_sem=fs_recv.at[slot],
                device_id=at(x + 1, core, z), device_id_type=MESH),
            pltpu.make_async_remote_copy(
                src_ref=yt_all.at[slot], dst_ref=yt_all.at[slot],
                send_sem=fy_send.at[slot], recv_sem=fy_recv.at[slot],
                device_id=at(x + 1, core, z), device_id_type=MESH),
        )

    sig_all[mine] = sig_ref[...]
    yt_all[mine] = yt_own[z]
    pass_on(z, lambda copy: copy.start())
    for d in range(1, Z):
        y_copy(d).start()

    is_first = lax.broadcasted_iota(jnp.int32, (C, 1), 0) < cols

    def spread(a0, a1):
        return jnp.where(is_first, a0, a1)

    def exchange(s, k):
        return pltpu.make_async_remote_copy(
            src_ref=own.at[s, k], dst_ref=got.at[s, k],
            send_sem=ex_send.at[s, k], recv_sem=ex_recv.at[s, k],
            device_id=at(x, 1 - core, z), device_id_type=MESH)

    def count_copy():
        return pltpu.make_async_remote_copy(
            src_ref=totals, dst_ref=got_totals, send_sem=t_send, recv_sem=t_recv,
            device_id=at(x, 1 - core, z), device_id_type=MESH)

    inner = jnp.minimum(z, Z - 1 - z)
    rest = jnp.where(2 * z >= Z, -1, 1)

    def nearest(i):
        near = jnp.where(i % 2 == 1, -((i + 1) // 2), i // 2)
        return z + jnp.where(i <= 2 * inner, near, rest * (i - inner))

    def block(i, dx):
        xx = x - dx
        zz = nearest(i)
        slot = xx * Z + zz
        is_last = (i == Z - 1) & (dx == x)

        @pl.when((dx == 0) & (i > 0))
        def _():
            hop(zz, 0).wait_recv()
            pass_on(zz, lambda copy: copy.start())
            y_arrival(zz).wait_recv()

        @pl.when(dx > 0)
        def _():
            for copy in upward(slot):
                copy.wait_recv()

        @pl.when(x < X - 1)
        def _():
            for copy in upward(slot):
                copy.start()

        base = pl.multiple_of(slot * rows, rows)
        live = yt_all[slot, cols:cols + MASK_ROWS, :].astype(f32)[0:1, :]
        y = yt_all[slot, 0:cols, :].astype(f32)
        for q in range(2):
            allow = jnp.where(2 * xx + core <= 2 * x + q, 1.0, 0.0).astype(f32)
            msk[q, :, pl.ds(base, rows)] = jnp.broadcast_to(live * allow, (8, rows))
            lhs[q * cols:(q + 1) * cols, :] = (y * allow).astype(jnp.bfloat16)

        @pl.when(is_last)
        def _():
            for q in range(2):
                total = jnp.sum(msk[q], axis=1, keepdims=True)
                totals[q] = jnp.broadcast_to(total, totals.shape[1:])
            count_copy().start()

        for k in range(nch):
            part = slice(k * chunk, (k + 1) * chunk)
            proj[:, part] = mm(sig_all[slot], w_ref[:, part])
        for k in range(nch):
            part = slice(k * chunk, (k + 1) * chunk)
            scale = sc_ref[:, part]
            phase = ph_ref[:, part]

            def strip(r, carry):
                r0 = pl.multiple_of(r * 16, 16)
                t = proj[pl.ds(r0, 16), part] * scale + phase
                f = t - ((t + ROUNDER) - ROUNDER)
                s = f * f
                acc = s * COS[-1] + COS[-2]
                for c in COS[-3::-1]:
                    acc = acc * s + c
                high, low = split(acc)
                to = pl.ds(pl.multiple_of(base + r0, 16), 16)
                hi[to, part] = high
                lo[to, part] = low
                return carry

            lax.fori_loop(0, rows // 16, strip, 0, unroll=4)
            here = pl.ds(base, rows)
            own[0, k] += mm(lhs[...], hi[here, part]) + mm(lhs[...], lo[here, part])

            @pl.when(is_last)
            def _():
                exchange(0, k).start()

    own[0] = jnp.zeros((nch, C, chunk), f32)

    def absent(slot, carry):
        here = pl.ds(pl.multiple_of(slot * rows, rows), rows)
        hi[here, :] = jnp.zeros((rows, F), jnp.bfloat16)
        lo[here, :] = jnp.zeros((rows, F), jnp.bfloat16)
        msk[:, :, here] = jnp.zeros((2, 8, rows), f32)
        return carry

    lax.fori_loop((x + 1) * Z, B, absent, 0)

    def column(i, carry):
        def one(dx, carry):
            block(i, dx)
            return carry

        return lax.fori_loop(0, x + 1, one, carry)

    lax.fori_loop(0, Z, column, 0)

    def passed(zz, carry):
        pass_on(zz, lambda copy: copy.wait_send())
        return carry

    lax.fori_loop(0, Z, passed, 0)
    for d in range(1, Z):
        y_copy(d).wait_send()

    @pl.when(x < X - 1)
    def _():
        def sent(slot, carry):
            for copy in upward(slot):
                copy.wait_send()
            return carry

        lax.fori_loop(0, (x + 1) * Z, sent, 0)

    count_copy().wait()
    count = [totals[q][0:1, 0:1] + got_totals[q][0:1, 0:1] for q in range(2)]
    inverse = spread(1.0 / count[0], 1.0 / count[1])

    width = F // Z
    first = pl.multiple_of(core * cols, cols)

    def piece(s, d):
        zz = lax.rem(z + d, Z)
        columns = pl.ds(pl.multiple_of(zz * width, width), width)
        return pltpu.make_async_remote_copy(
            src_ref=vec.at[s, pl.ds(first, cols), columns], dst_ref=landing.at[s, z],
            send_sem=o_send.at[s, d], recv_sem=o_recv.at[s, d],
            device_id=at(x, core, zz), device_id_type=MESH)

    def send_pieces(s):
        for d in range(1, Z):
            piece(s, d).start()
        columns = pl.ds(pl.multiple_of(z * width, width), width)
        landing[s, z] = vec[s, pl.ds(first, cols), columns]

    def keep(v, part):
        high, low = split(v.T)
        vs[part, 0:C] = high
        vs[part, C:2 * C] = low

    def forward(to):
        def one(j, carry):
            here = pl.ds(pl.multiple_of(j * band, band), band)
            u = mm(hi[here, :], vs[...])
            u = (u[:, 0:C] + u[:, C:]).T
            to[0:cols, here] = u[0:cols] * msk[0, 0:1, here]
            to[cols:C, here] = u[cols:] * msk[1, 0:1, here]
            return carry

        lax.fori_loop(0, n // band, one, 0)

    norm = jnp.zeros((C, 1), f32)
    for k in range(nch):
        part = slice(k * chunk, (k + 1) * chunk)
        exchange(0, k).wait()
        v = (own[0, k] + got[0, k]) * inverse
        vec[0, :, part] = v
        keep(v, part)
        norm = norm + jnp.sum(v * v, axis=1, keepdims=True)
    send_pieces(0)
    forward(u_now)

    tile_row = lax.broadcasted_iota(jnp.int32, (8, 128), 0)

    def tile(norm, curve):
        out = jnp.zeros((8, 128), f32)
        for i, a in enumerate((norm[0:cols], norm[cols:], curve[0:cols], curve[cols:])):
            out = jnp.where(tile_row == i, jnp.sum(a, axis=0, keepdims=True), out)
        return out

    steps = []
    for it in range(ITERS - 1):
        s = it + 1
        for k in range(n // chunk):
            part = slice(k * chunk, (k + 1) * chunk)
            high, low = split(u_now[:, part])
            ust[0:C, part] = high
            ust[C:2 * C, part] = low
        for k in range(nch):
            part = slice(k * chunk, (k + 1) * chunk)
            image = mm(ust[...], hi[:, part])
            own[s, k] = image[0:C] + image[C:] + mm(ust[0:C, :], lo[:, part])
            exchange(s, k).start()
        curve = jnp.zeros((C, 1), f32)
        for k in range(nch):
            part = slice(k * chunk, (k + 1) * chunk)
            exchange(s, k).wait()
            v = res[:, part] if it else vec[0, :, part]
            image = (own[s, k] + got[s, k]) * inverse + ridge_penalty * v
            vec[s, :, part] = image
            keep(image, part)
            curve = curve + jnp.sum(v * image, axis=1, keepdims=True)
        scal[it, z] = tile(norm, curve)
        copies = []
        for d in range(1, Z):
            copies.append(pltpu.make_async_remote_copy(
                src_ref=scal.at[it, z], dst_ref=scal.at[it, z],
                send_sem=sc_send.at[it, d], recv_sem=sc_recv.at[it, d],
                device_id=at(x, core, lax.rem(z + d, Z)), device_id_type=MESH))
        for copy in copies:
            copy.start()
        send_pieces(s)
        forward(u_image)
        for copy in copies:
            copy.wait()
        a = scal[it, 0]
        for i in range(1, Z):
            a = a + scal[it, i]
        res_norm = spread(a[0:1, 0:1], a[1:2, 0:1])
        res_curve = spread(a[2:3, 0:1], a[3:4, 0:1])
        step = res_norm / entries / (res_curve / entries + epsilon)
        steps.append(step)
        norm = jnp.zeros((C, 1), f32)
        for k in range(nch):
            part = slice(k * chunk, (k + 1) * chunk)
            v = res[:, part] if it else vec[0, :, part]
            v = v - step * vec[s, :, part]
            res[:, part] = v
            norm = norm + jnp.sum(v * v, axis=1, keepdims=True)
        square = jnp.zeros((C, 1), f32)
        for k in range(n // chunk):
            part = slice(k * chunk, (k + 1) * chunk)
            u = u_now[:, part] - step * u_image[:, part]
            u_now[:, part] = u
            square = square + jnp.sum(u * u, axis=1, keepdims=True)

    last[core * Z + z] = tile(norm, square)
    copies = []
    for d in range(1, 2 * Z):
        cc, zz = lax.rem(core + d // Z, 2), lax.rem(z + d % Z, Z)
        copies.append(pltpu.make_async_remote_copy(
            src_ref=last.at[core * Z + z], dst_ref=last.at[core * Z + z],
            send_sem=la_send.at[d], recv_sem=la_recv.at[d],
            device_id=at(x, cc, zz), device_id_type=MESH))
    for copy in copies:
        copy.start()
    for copy in copies:
        copy.wait()
    a = last[0]
    for i in range(1, 2 * Z):
        a = a + last[i]
    norms = spread(a[0:1, 0:1], a[1:2, 0:1]) * 0.5
    curve = spread(a[2:3, 0:1] / count[0], a[3:4, 0:1] / count[1]) + ridge_penalty * norms
    steps.append(norms / entries / (curve / entries + epsilon))

    def here_of(column):
        return jnp.where(core == 0, column[0:1], column[cols:cols + 1])

    root = here_of(spread(jnp.sqrt(count[0]), jnp.sqrt(count[1])))
    s0, s1, s2 = [here_of(step) for step in steps]
    for s in range(ITERS):
        for d in range(1, Z):
            piece(s, d).wait()
    for i in range(Z):
        coef = (s0 + s1 + s2) * landing[0, i] - (s1 + s2) * s0 * landing[1, i]
        coef = coef - s1 * s2 * landing[2, i]
        outbox[i * cols:(i + 1) * cols, :] = coef * root
    out_ref[...] = outbox[...].T


def scratch_of(X, Z, rows, K, F, cols, chunk):
    B = X * Z
    n = B * rows
    C = 2 * cols
    nch = F // chunk
    f32, bf16 = jnp.float32, jnp.bfloat16
    buffers = [
        ((Z, cols + MASK_ROWS, rows), bf16), ((1, F), f32), ((1, F), f32),
        ((B, rows, K), bf16), ((B, cols + MASK_ROWS, rows), bf16),
        ((n, F), bf16), ((n, F), bf16), ((rows, F), f32), ((C, rows), bf16),
        ((2, 8, n), f32), ((ITERS, C, F), f32), ((C, F), f32),
        ((C, n), f32), ((C, n), f32), ((F, 2 * C), bf16), ((2 * C, n), bf16),
        ((ITERS, nch, C, chunk), f32), ((ITERS, nch, C, chunk), f32),
        ((2, 8, 128), f32), ((2, 8, 128), f32),
        ((ITERS, Z, 8, 128), f32), ((2 * Z, 8, 128), f32),
        ((Z * cols, F // Z), f32), ((ITERS, Z, cols, F // Z), f32),
    ]
    held = sum(math.prod(shape) * jnp.dtype(dtype).itemsize for shape, dtype in buffers)
    sems = [(2, Z)] + [(Z,)] * 3 + [(B,)] * 4 + [(ITERS, nch)] * 2 + [()] * 2 + [(ITERS, Z)] * 2 + [(2 * Z,)] * 2 + [(ITERS, Z)] * 2
    return buffers, sems, held


VMEM_BUDGET = 44 * 2**20


def plan(E, Z, rows, K, F, T):
    if E % 2 or T % Z or F % Z:
        return None
    cols, chunk = T // Z, 512
    n_bad = (E // 2 * Z * rows) % chunk
    if (E // 2 * Z) % 2 or ITERS != 3 or n_bad or cols % 16 or rows % 128 or F % chunk or (F // Z) % 128 or K % 128:
        return None
    buffers, sems, held = scratch_of(E // 2, Z, rows, K, F, cols, chunk)
    if held > VMEM_BUDGET:
        return None
    return cols, chunk, buffers, sems


def fused(signals, targets, row_counts, feature_weights, phases, spread_ids):
    E, Z = lax.axis_size("epoch"), lax.axis_size("asset")
    rows, K = signals.shape[1:]
    F = feature_weights.shape[1]
    T = targets.shape[2]
    cols, chunk, buffers, sems = plan(E, Z, rows, K, F, T)
    vmem = pl.BlockSpec(memory_space=pltpu.VMEM)
    out = pl.pallas_call(
        functools.partial(kernel, E // 2, Z, chunk, float(F * T)),
        out_shape=jax.ShapeDtypeStruct((F // Z, T), jnp.float32),
        in_specs=[pl.BlockSpec(memory_space=pltpu.SMEM)] + [vmem] * 5,
        out_specs=vmem,
        scratch_shapes=[pltpu.VMEM(s, d) for s, d in buffers]
        + [pltpu.SemaphoreType.DMA(s) if s else pltpu.SemaphoreType.DMA for s in sems],
        compiler_params=pltpu.CompilerParams(
            collective_id=0, has_side_effects=True, vmem_limit_bytes=56 * 2**20),
    )(row_counts, signals[0], targets[0], feature_weights, spread_ids[None, :], phases[None, :])
    return out[None]


def solution(mesh):
    def run(signals, targets, row_counts, feature_weights, phases, spread_ids):
        fits = plan(
            mesh.shape["epoch"], mesh.shape["asset"], signals.shape[1],
            signals.shape[2], feature_weights.shape[1], targets.shape[2])
        body = fused if fits else on_device
        return body(signals, targets, row_counts, feature_weights, phases, spread_ids)

    placed = (
        P(("grp", "epoch"), "asset", None),
        P(("grp", "epoch"), "asset", None),
        P(("grp", "epoch"), "asset"),
        P(),
        P(),
        P(),
    )
    return jax.shard_map(
        run,
        mesh=mesh,
        in_specs=placed,
        out_specs=P(("grp", "epoch"), "asset", None),
        check_vma=False,
    )
```

```python
import functools
import math

import jax
import jax.numpy as jnp
from jax import lax
from jax.experimental import pallas as pl
from jax.experimental.pallas import tpu as pltpu
from jax.sharding import PartitionSpec as P

ITERS = 3


ridge_penalty = 0.05
epsilon = 1e-06


def prefix(part, axis, combine, identity):
    place = lax.axis_index(axis)
    gathered = jax.tree.map(lambda a: lax.all_gather(a, axis), part)
    state = jax.tree.map(lambda a, e: jnp.zeros_like(a) + jnp.asarray(e, a.dtype), part, identity)

    def one(hop, state):
        return combine(
            state, jax.tree.map(lambda a: lax.dynamic_index_in_dim(a, hop, 0, False), gathered)
        )

    return lax.fori_loop(0, place, one, state)


def feature_scale(spread_ids):
    return (
        0.5
        * (
            1.0
            + jnp.where(spread_ids >= 1, 1.0, 0.0)
            + jnp.where(spread_ids >= 2, 2.0, 0.0)
            + jnp.where(spread_ids >= 3, 4.0, 0.0)
        )
    ).astype(jnp.float32)


def make_features(inputs, feature_weights, phases, spread_ids):
    projected = jnp.dot(inputs, feature_weights, preferred_element_type=jnp.float32)
    return jnp.sin(projected * feature_scale(spread_ids) + phases)


def add_pair(earlier, later):
    return (earlier[0] + later[0], earlier[1] + later[1])


def on_device(signals, targets, row_counts, feature_weights, phases, spread_ids):
    rows = signals.shape[1]
    width = feature_weights.shape[1]
    tgt_width = targets.shape[2]
    groups = lax.axis_size("asset")
    block_size = width // groups
    entries = width * tgt_width
    own_rows = row_counts[0, 0]
    all_counts = lax.all_gather(row_counts[0], "asset", axis=0, tiled=True)
    row_sum = jnp.sum(all_counts).astype(jnp.float32)
    inputs = signals[0]
    returns = targets[0]
    features = make_features(inputs, feature_weights, phases, spread_ids)
    live_mask = (jnp.arange(rows) < own_rows)[:, None]
    features = jnp.where(live_mask, features, jnp.zeros_like(features))
    returns = jnp.where(live_mask, returns.astype(jnp.float32), jnp.zeros((), jnp.float32))
    combined = jnp.concatenate([features, returns], axis=1)
    contract_rows = (((0,), (0,)), ((), ()))
    gram_block = lax.psum_scatter(
        lax.dot_general(features, combined, contract_rows, precision=lax.Precision.HIGHEST),
        "asset",
        scatter_dimension=0,
        tiled=True,
    )
    earlier, earlier_rows = prefix(
        (gram_block, row_sum),
        "epoch",
        add_pair,
        (jnp.zeros_like(gram_block), jnp.zeros((), jnp.float32)),
    )
    cumulative = earlier + gram_block
    row_total = earlier_rows + row_sum
    first_row = lax.axis_index("asset") * block_size
    diagonal = jnp.arange(width)[None, :] == first_row + jnp.arange(block_size)[:, None]
    system = cumulative[:, :width] / row_total + ridge_penalty * jnp.where(
        diagonal, 1.0, 0.0
    ).astype(jnp.float32)
    residual = cumulative[:, width:] / row_total
    coef = jnp.zeros((block_size, tgt_width), jnp.float32)
    for iteration in range(ITERS):
        image = jnp.zeros((block_size, tgt_width), jnp.float32) + jnp.dot(
            system,
            lax.all_gather(residual, "asset", axis=0, tiled=True),
            precision=lax.Precision.HIGHEST,
        )
        res_norm, res_curve = lax.psum(
            (jnp.sum(residual * residual), jnp.sum(residual * image)), "asset"
        )
        step_size = res_norm / entries / (res_curve / entries + epsilon)
        coef = coef + step_size * residual
        residual = residual - step_size * image
    return (jnp.sqrt(row_total) * coef)[None]


MESH = pl.DeviceIdType.MESH
MASK_ROWS = 16
COS = (
    0.9999992251396179,
    -19.738977432250977,
    64.9285888671875,
    -85.27084350585938,
    58.78694152832031,
    -21.0654296875,
)
ROUNDER = 1.5 * 2.0**23
def mm(a, b):
    return jnp.dot(a, b, preferred_element_type=jnp.float32)


def split(a):
    high = a.astype(jnp.bfloat16)
    return high, (a - high.astype(jnp.float32)).astype(jnp.bfloat16)


def kernel(
    X, Z, chunk, entries,
    counts_ref, sig_ref, y_ref, w_ref, ids_ref, phases_ref, out_ref,
    yt_own, sc_ref, ph_ref,
    sig_all, yt_all, hi, lo, proj, lhs, msk, vec, res, u_now, u_image, vs, ust, own, got, totals, got_totals,
    scal, last, outbox, landing,
    gs_send, gs_recv, gy_send, gy_recv, fs_send, fs_recv, fy_send, fy_recv,
    ex_send, ex_recv, t_send, t_recv,
    sc_send, sc_recv, la_send, la_recv, o_send, o_recv,
):
    rows, K = sig_ref.shape
    F = w_ref.shape[1]
    cols = y_ref.shape[1] // Z
    C = 2 * cols
    B = X * Z
    n = B * rows
    nch = F // chunk
    band = 2 * rows
    f32 = jnp.float32
    epoch = lax.axis_index("epoch")
    z = lax.axis_index("asset")
    x = epoch // 2
    core = epoch % 2

    def at(xx, cc, zz):
        return {"epoch": 2 * xx + cc, "asset": zz}

    def signal(peer):
        pl.semaphore_signal(barrier, inc=1, device_id=peer, device_id_type=MESH)

    barrier = pltpu.get_barrier_semaphore()
    for d in range(1, Z):
        signal(at(x, core, lax.rem(z + d, Z)))
    for d in range(Z):
        signal(at(x, 1 - core, lax.rem(z + d, Z)))

    beside = sorted({1 % X, X - 1} - {0})
    for d in beside:
        signal(at(lax.rem(x + d, X), core, z))

    count_here = counts_ref[0, 0]
    alive = lax.broadcasted_iota(jnp.int32, (rows, 1), 0) < count_here
    y = jnp.where(alive, y_ref[...].astype(f32), 0.0).T
    alive = lax.broadcasted_iota(jnp.int32, (MASK_ROWS, rows), 1) < count_here
    mask = jnp.where(alive, 1.0, 0.0).astype(jnp.bfloat16)
    for b in range(Z):
        yt_own[b, 0:cols, :] = y[b * cols:(b + 1) * cols].astype(jnp.bfloat16)
        yt_own[b, cols:cols + MASK_ROWS, :] = mask
    turn = 1.0 / (2.0 * math.pi)
    sc_ref[...] = feature_scale(ids_ref[...]) * turn
    ph_ref[...] = phases_ref[...] * turn - 0.25

    pl.semaphore_wait(barrier, 2 * Z - 1 + len(beside))

    mine = x * Z + z

    def hop(zz, way):
        slot = x * Z + zz
        return pltpu.make_async_remote_copy(
            src_ref=sig_all.at[slot], dst_ref=sig_all.at[slot],
            send_sem=gs_send.at[way, zz], recv_sem=gs_recv.at[zz],
            device_id=at(x, core, lax.rem(z + 2 * way - 1 + Z, Z)), device_id_type=MESH)

    def y_copy(d):
        zz = lax.rem(z + d, Z)
        return pltpu.make_async_remote_copy(
            src_ref=yt_own.at[zz], dst_ref=yt_all.at[mine],
            send_sem=gy_send.at[d], recv_sem=gy_recv.at[z],
            device_id=at(x, core, zz), device_id_type=MESH)

    def y_arrival(zz):
        return pltpu.make_async_remote_copy(
            src_ref=yt_own.at[zz], dst_ref=yt_all.at[x * Z + zz],
            send_sem=gy_send.at[0], recv_sem=gy_recv.at[zz],
            device_id=at(x, core, zz), device_id_type=MESH)

    def pass_on(zz, act):
        @pl.when((zz <= z) & (z < Z - 1))
        def _():
            act(hop(zz, 1))

        @pl.when((zz >= z) & (z > 0))
        def _():
            act(hop(zz, 0))

    def upward(slot):
        return (
            pltpu.make_async_remote_copy(
                src_ref=sig_all.at[slot], dst_ref=sig_all.at[slot],
                send_sem=fs_send.at[slot], recv_sem=fs_recv.at[slot],
                device_id=at(x + 1, core, z), device_id_type=MESH),
            pltpu.make_async_remote_copy(
                src_ref=yt_all.at[slot], dst_ref=yt_all.at[slot],
                send_sem=fy_send.at[slot], recv_sem=fy_recv.at[slot],
                device_id=at(x + 1, core, z), device_id_type=MESH),
        )

    sig_all[mine] = sig_ref[...]
    yt_all[mine] = yt_own[z]
    pass_on(z, lambda copy: copy.start())
    for d in range(1, Z):
        y_copy(d).start()

    is_first = lax.broadcasted_iota(jnp.int32, (C, 1), 0) < cols

    def spread(a0, a1):
        return jnp.where(is_first, a0, a1)

    def exchange(s, k):
        return pltpu.make_async_remote_copy(
            src_ref=own.at[s, k], dst_ref=got.at[s, k],
            send_sem=ex_send.at[s, k], recv_sem=ex_recv.at[s, k],
            device_id=at(x, 1 - core, z), device_id_type=MESH)

    def count_copy():
        return pltpu.make_async_remote_copy(
            src_ref=totals, dst_ref=got_totals, send_sem=t_send, recv_sem=t_recv,
            device_id=at(x, 1 - core, z), device_id_type=MESH)

    inner = jnp.minimum(z, Z - 1 - z)
    rest = jnp.where(2 * z >= Z, -1, 1)

    def nearest(i):
        near = jnp.where(i % 2 == 1, -((i + 1) // 2), i // 2)
        return z + jnp.where(i <= 2 * inner, near, rest * (i - inner))

    def block(i, dx):
        xx = x - dx
        zz = nearest(i)
        slot = xx * Z + zz
        is_last = (i == Z - 1) & (dx == x)

        @pl.when((dx == 0) & (i > 0))
        def _():
            hop(zz, 0).wait_recv()
            pass_on(zz, lambda copy: copy.start())
            y_arrival(zz).wait_recv()

        @pl.when(dx > 0)
        def _():
            for copy in upward(slot):
                copy.wait_recv()

        @pl.when(x < X - 1)
        def _():
            for copy in upward(slot):
                copy.start()

        base = pl.multiple_of(slot * rows, rows)
        live = yt_all[slot, cols:cols + MASK_ROWS, :].astype(f32)[0:1, :]
        y = yt_all[slot, 0:cols, :].astype(f32)
        for q in range(2):
            allow = jnp.where(2 * xx + core <= 2 * x + q, 1.0, 0.0).astype(f32)
            msk[q, :, pl.ds(base, rows)] = jnp.broadcast_to(live * allow, (8, rows))
            lhs[q * cols:(q + 1) * cols, :] = (y * allow).astype(jnp.bfloat16)

        @pl.when(is_last)
        def _():
            for q in range(2):
                total = jnp.sum(msk[q], axis=1, keepdims=True)
                totals[q] = jnp.broadcast_to(total, totals.shape[1:])
            count_copy().start()

        for k in range(nch):
            part = slice(k * chunk, (k + 1) * chunk)
            proj[:, part] = mm(sig_all[slot], w_ref[:, part])
        for k in range(nch):
            part = slice(k * chunk, (k + 1) * chunk)
            scale = sc_ref[:, part]
            phase = ph_ref[:, part]

            def strip(r, carry):
                r0 = pl.multiple_of(r * 16, 16)
                t = proj[pl.ds(r0, 16), part] * scale + phase
                f = t - ((t + ROUNDER) - ROUNDER)
                s = f * f
                acc = s * COS[-1] + COS[-2]
                for c in COS[-3::-1]:
                    acc = acc * s + c
                high, low = split(acc)
                to = pl.ds(pl.multiple_of(base + r0, 16), 16)
                hi[to, part] = high
                lo[to, part] = low
                return carry

            lax.fori_loop(0, rows // 16, strip, 0, unroll=rows // 16)
            here = pl.ds(base, rows)
            own[0, k] += mm(lhs[...], hi[here, part]) + mm(lhs[...], lo[here, part])

        @pl.when(is_last)
        def _():
            for k in range(nch):
                exchange(0, k).start()

    own[0] = jnp.zeros((nch, C, chunk), f32)

    def absent(slot, carry):
        here = pl.ds(pl.multiple_of(slot * rows, rows), rows)
        hi[here, :] = jnp.zeros((rows, F), jnp.bfloat16)
        lo[here, :] = jnp.zeros((rows, F), jnp.bfloat16)
        msk[:, :, here] = jnp.zeros((2, 8, rows), f32)
        return carry

    lax.fori_loop((x + 1) * Z, B, absent, 0)

    def column(i, carry):
        def one(dx, carry):
            block(i, dx)
            return carry

        return lax.fori_loop(0, x + 1, one, carry)

    lax.fori_loop(0, Z, column, 0)

    def passed(zz, carry):
        pass_on(zz, lambda copy: copy.wait_send())
        return carry

    lax.fori_loop(0, Z, passed, 0)
    for d in range(1, Z):
        y_copy(d).wait_send()

    @pl.when(x < X - 1)
    def _():
        def sent(slot, carry):
            for copy in upward(slot):
                copy.wait_send()
            return carry

        lax.fori_loop(0, (x + 1) * Z, sent, 0)

    count_copy().wait()
    count = [totals[q][0:1, 0:1] + got_totals[q][0:1, 0:1] for q in range(2)]
    inverse = spread(1.0 / count[0], 1.0 / count[1])

    width = F // Z
    first = pl.multiple_of(core * cols, cols)

    def piece(s, d):
        zz = lax.rem(z + d, Z)
        columns = pl.ds(pl.multiple_of(zz * width, width), width)
        return pltpu.make_async_remote_copy(
            src_ref=vec.at[s, pl.ds(first, cols), columns], dst_ref=landing.at[s, z],
            send_sem=o_send.at[s, d], recv_sem=o_recv.at[s, d],
            device_id=at(x, core, zz), device_id_type=MESH)

    def send_pieces(s):
        for d in range(1, Z):
            piece(s, d).start()
        columns = pl.ds(pl.multiple_of(z * width, width), width)
        landing[s, z] = vec[s, pl.ds(first, cols), columns]

    def keep(v, part):
        high, low = split(v.T)
        vs[part, 0:C] = high
        vs[part, C:2 * C] = low

    def forward(to):
        def one(j, carry):
            here = pl.ds(pl.multiple_of(j * band, band), band)
            u = mm(hi[here, :], vs[...])
            u = (u[:, 0:C] + u[:, C:]).T
            to[0:cols, here] = u[0:cols] * msk[0, 0:1, here]
            to[cols:C, here] = u[cols:] * msk[1, 0:1, here]
            return carry

        lax.fori_loop(0, n // band, one, 0)

    norm = jnp.zeros((C, 1), f32)
    for k in range(nch):
        part = slice(k * chunk, (k + 1) * chunk)
        exchange(0, k).wait()
        v = (own[0, k] + got[0, k]) * inverse
        vec[0, :, part] = v
        keep(v, part)
        norm = norm + jnp.sum(v * v, axis=1, keepdims=True)
    send_pieces(0)
    forward(u_now)

    tile_row = lax.broadcasted_iota(jnp.int32, (8, 128), 0)

    def tile(norm, curve):
        out = jnp.zeros((8, 128), f32)
        for i, a in enumerate((norm[0:cols], norm[cols:], curve[0:cols], curve[cols:])):
            out = jnp.where(tile_row == i, jnp.sum(a, axis=0, keepdims=True), out)
        return out

    steps = []
    for it in range(ITERS - 1):
        s = it + 1
        for k in range(n // chunk):
            part = slice(k * chunk, (k + 1) * chunk)
            high, low = split(u_now[:, part])
            ust[0:C, part] = high
            if it == 0:
                ust[C:2 * C, part] = low
        for k in range(nch):
            part = slice(k * chunk, (k + 1) * chunk)
            if it == 0:
                image = mm(ust[...], hi[:, part])
                own[s, k] = image[0:C] + image[C:] + mm(ust[0:C, :], lo[:, part])
            else:
                own[s, k] = mm(ust[0:C, :], hi[:, part])
            exchange(s, k).start()
        curve = jnp.zeros((C, 1), f32)
        for k in range(nch):
            part = slice(k * chunk, (k + 1) * chunk)
            exchange(s, k).wait()
            v = res[:, part] if it else vec[0, :, part]
            image = (own[s, k] + got[s, k]) * inverse + ridge_penalty * v
            vec[s, :, part] = image
            keep(image, part)
            curve = curve + jnp.sum(v * image, axis=1, keepdims=True)
        scal[it, z] = tile(norm, curve)
        copies = []
        for d in range(1, Z):
            copies.append(pltpu.make_async_remote_copy(
                src_ref=scal.at[it, z], dst_ref=scal.at[it, z],
                send_sem=sc_send.at[it, d], recv_sem=sc_recv.at[it, d],
                device_id=at(x, core, lax.rem(z + d, Z)), device_id_type=MESH))
        for copy in copies:
            copy.start()
        send_pieces(s)
        forward(u_image)
        for copy in copies:
            copy.wait()
        a = scal[it, 0]
        for i in range(1, Z):
            a = a + scal[it, i]
        res_norm = spread(a[0:1, 0:1], a[1:2, 0:1])
        res_curve = spread(a[2:3, 0:1], a[3:4, 0:1])
        step = res_norm / entries / (res_curve / entries + epsilon)
        steps.append(step)
        norm = jnp.zeros((C, 1), f32)
        for k in range(nch):
            part = slice(k * chunk, (k + 1) * chunk)
            v = res[:, part] if it else vec[0, :, part]
            v = v - step * vec[s, :, part]
            res[:, part] = v
            norm = norm + jnp.sum(v * v, axis=1, keepdims=True)
        square = jnp.zeros((C, 1), f32)
        for k in range(n // chunk):
            part = slice(k * chunk, (k + 1) * chunk)
            u = u_now[:, part] - step * u_image[:, part]
            u_now[:, part] = u
            square = square + jnp.sum(u * u, axis=1, keepdims=True)

    last[core * Z + z] = tile(norm, square)
    copies = []
    for d in range(1, 2 * Z):
        cc, zz = lax.rem(core + d // Z, 2), lax.rem(z + d % Z, Z)
        copies.append(pltpu.make_async_remote_copy(
            src_ref=last.at[core * Z + z], dst_ref=last.at[core * Z + z],
            send_sem=la_send.at[d], recv_sem=la_recv.at[d],
            device_id=at(x, cc, zz), device_id_type=MESH))
    for copy in copies:
        copy.start()
    for copy in copies:
        copy.wait()
    a = last[0]
    for i in range(1, 2 * Z):
        a = a + last[i]
    norms = spread(a[0:1, 0:1], a[1:2, 0:1]) * 0.5
    curve = spread(a[2:3, 0:1] / count[0], a[3:4, 0:1] / count[1]) + ridge_penalty * norms
    steps.append(norms / entries / (curve / entries + epsilon))

    def here_of(column):
        return jnp.where(core == 0, column[0:1], column[cols:cols + 1])

    root = here_of(spread(jnp.sqrt(count[0]), jnp.sqrt(count[1])))
    s0, s1, s2 = [here_of(step) for step in steps]
    for s in range(ITERS):
        for d in range(1, Z):
            piece(s, d).wait()
    for i in range(Z):
        coef = (s0 + s1 + s2) * landing[0, i] - (s1 + s2) * s0 * landing[1, i]
        coef = coef - s1 * s2 * landing[2, i]
        outbox[i * cols:(i + 1) * cols, :] = coef * root
    out_ref[...] = outbox[...].T


def scratch_of(X, Z, rows, K, F, cols, chunk):
    B = X * Z
    n = B * rows
    C = 2 * cols
    nch = F // chunk
    f32, bf16 = jnp.float32, jnp.bfloat16
    buffers = [
        ((Z, cols + MASK_ROWS, rows), bf16), ((1, F), f32), ((1, F), f32),
        ((B, rows, K), bf16), ((B, cols + MASK_ROWS, rows), bf16),
        ((n, F), bf16), ((n, F), bf16), ((rows, F), f32), ((C, rows), bf16),
        ((2, 8, n), f32), ((ITERS, C, F), f32), ((C, F), f32),
        ((C, n), f32), ((C, n), f32), ((F, 2 * C), bf16), ((2 * C, n), bf16),
        ((ITERS, nch, C, chunk), f32), ((ITERS, nch, C, chunk), f32),
        ((2, 8, 128), f32), ((2, 8, 128), f32),
        ((ITERS, Z, 8, 128), f32), ((2 * Z, 8, 128), f32),
        ((Z * cols, F // Z), f32), ((ITERS, Z, cols, F // Z), f32),
    ]
    held = sum(math.prod(shape) * jnp.dtype(dtype).itemsize for shape, dtype in buffers)
    sems = [(2, Z)] + [(Z,)] * 3 + [(B,)] * 4 + [(ITERS, nch)] * 2 + [()] * 2 + [(ITERS, Z)] * 2 + [(2 * Z,)] * 2 + [(ITERS, Z)] * 2
    return buffers, sems, held


VMEM_BUDGET = 44 * 2**20


def plan(E, Z, rows, K, F, T):
    if E % 2 or T % Z or F % Z:
        return None
    cols, chunk = T // Z, 512
    n_bad = (E // 2 * Z * rows) % chunk
    if (E // 2 * Z) % 2 or ITERS != 3 or n_bad or cols % 16 or rows % 128 or F % chunk or (F // Z) % 128 or K % 128:
        return None
    buffers, sems, held = scratch_of(E // 2, Z, rows, K, F, cols, chunk)
    if held > VMEM_BUDGET:
        return None
    return cols, chunk, buffers, sems


def fused(signals, targets, row_counts, feature_weights, phases, spread_ids):
    E, Z = lax.axis_size("epoch"), lax.axis_size("asset")
    rows, K = signals.shape[1:]
    F = feature_weights.shape[1]
    T = targets.shape[2]
    cols, chunk, buffers, sems = plan(E, Z, rows, K, F, T)
    vmem = pl.BlockSpec(memory_space=pltpu.VMEM)
    out = pl.pallas_call(
        functools.partial(kernel, E // 2, Z, chunk, float(F * T)),
        out_shape=jax.ShapeDtypeStruct((F // Z, T), jnp.float32),
        in_specs=[pl.BlockSpec(memory_space=pltpu.SMEM)] + [vmem] * 5,
        out_specs=vmem,
        scratch_shapes=[pltpu.VMEM(s, d) for s, d in buffers]
        + [pltpu.SemaphoreType.DMA(s) if s else pltpu.SemaphoreType.DMA for s in sems],
        compiler_params=pltpu.CompilerParams(
            collective_id=0, has_side_effects=True, vmem_limit_bytes=56 * 2**20),
    )(row_counts, signals[0], targets[0], feature_weights, spread_ids[None, :], phases[None, :])
    return out[None]


def solution(mesh):
    def run(signals, targets, row_counts, feature_weights, phases, spread_ids):
        fits = plan(
            mesh.shape["epoch"], mesh.shape["asset"], signals.shape[1],
            signals.shape[2], feature_weights.shape[1], targets.shape[2])
        body = fused if fits else on_device
        return body(signals, targets, row_counts, feature_weights, phases, spread_ids)

    placed = (
        P(("grp", "epoch"), "asset", None),
        P(("grp", "epoch"), "asset", None),
        P(("grp", "epoch"), "asset"),
        P(),
        P(),
        P(),
    )
    return jax.shard_map(
        run,
        mesh=mesh,
        in_specs=placed,
        out_specs=P(("grp", "epoch"), "asset", None),
        check_vma=False,
    )
```
